32 devices in a mesh: fsdp: 8 (over z, y), et: 4 (over x, core).
Axes of the slice: x: 2, y: 2, z: 4, core: 2. Of those that a mesh axis runs over, the one named last changes fastest.
Arguments:
- tokens: bfloat16 [4096, 3072], P(('fsdp', 'et')), may hold values from -6 to 6
- cotangent: bfloat16 [4096, 3072], P(('fsdp', 'et')), may hold values from -6 to 6
- route_experts: int32 [4096, 2], P('fsdp'), may hold values from 0 to 7, as said below
- route_gates: float32 [4096, 2], P('fsdp'), may hold values from 0.2 to 1
- w_gate: bfloat16 [3072, 8192], P('fsdp', 'et'), may hold values from -0.109375 to 0.109375
- w_up: bfloat16 [3072, 8192], P('fsdp', 'et'), may hold values from -0.109375 to 0.109375
- w_down: bfloat16 [8192, 3072], P('et', 'fsdp'), may hold values from -0.0625 to 0.0625
Outputs:
- moe_out: bfloat16 [4096, 3072], P(('fsdp', 'et'))
- grad_tokens: bfloat16 [4096, 3072], P(('fsdp', 'et'))
The draws below stay inside these ranges and needn't reach their ends.
Inputs may be any that keep to these rules, and one draw needn't show every extreme that they name: `route_experts`: each row names two different experts. Among the 128 rows of one device (aligned blocks of rows) at most 16 name expert 0, so a group of 512 rows has at most 64 such rows; in every draw some device reaches 16 and some group reaches 64.
All inputs are finite; a program needn't handle non-finite values.
Results may differ from the reference program's by a relative error of at most 0.024.
Values may be sent and summed in bfloat16 or wider, within the bound.
No kernel may reach another device: no remote copies, remote signals or barrier semaphores. Data moves between devices by JAX's collectives and lax.ppermute only.
A program may use at most 128 MiB of HBM per device.

```python
import jax
import jax.numpy as jnp
from jax import lax

D = 3072
FF = 8192
EXPERTS = 8
TOK_DEV = 128
DEV_MOST = 16
GROUP = 512
CAP = 64
TOKENS = 4096
N_FSDP = 8
N_ET = 4


def draw_route_experts(key, part):
    blocks = TOKENS // TOK_DEV
    per_group = GROUP // TOK_DEV
    key_list = jax.random.split(key, 6)
    lowest = max(1, DEV_MOST // 3)
    counts = jax.random.randint(key_list[0], (blocks,), lowest, DEV_MOST + 1)
    fullest = jax.random.randint(key_list[1], (), 0, TOKENS // GROUP)
    block_group = jnp.arange(blocks) // per_group
    counts = jnp.where(block_group == fullest, DEV_MOST, counts)

    def one_order(sub_key):
        return jax.random.permutation(sub_key, TOK_DEV)
    ranking = jax.vmap(one_order)(jax.random.split(key_list[2], blocks))
    routed = ranking < counts[:, None]
    other_pick = jax.random.randint(key_list[3], (blocks, TOK_DEV), 1, EXPERTS)
    slot_side = jax.random.randint(key_list[4], (blocks, TOK_DEV), 0, 2)
    offset_pick = jax.random.randint(key_list[5], (blocks, TOK_DEV), 1, EXPERTS - 1)
    partner_pick = 1 + (other_pick - 1 + offset_pick) % (EXPERTS - 1)
    first_pick = jnp.where(routed, jnp.where(slot_side == 0, 0, other_pick), other_pick)
    second_pick = jnp.where(routed, jnp.where(slot_side == 0, other_pick, 0), partner_pick)
    return jnp.stack([first_pick, second_pick], axis=-1).reshape(TOKENS, 2).astype(jnp.int32)


def levels(key, shape, cuts, smallest, high):
    def one(axis_at, parts):
        steps = jax.random.uniform(jax.random.fold_in(jax.random.fold_in(key, 6), axis_at), (parts,), jnp.float32, smallest / len(cuts), high / len(cuts))
        return jnp.repeat(jnp.exp(steps), shape[axis_at] // parts).reshape((-1,) + (1,) * (len(shape) - axis_at - 1))

    gain = one(*cuts[0])
    for cut in cuts[1:]:
        gain = gain * one(*cut)
    return gain


def bell_draw(own_key, extent, scale, limit, shards=(), kind=jnp.bfloat16):
    values = jax.random.normal(own_key, extent, jnp.float32) * scale
    if len(shards) > 0:
        values = levels(own_key, extent, shards, -0.22, 0.18) * values
    return jnp.clip(values, min=-limit, max=limit).astype(kind)


def setup_inputs(seed: int = 0) -> dict:
    keys = jax.random.split(jax.random.key(seed), 8)
    return {
        "tokens": bell_draw(keys[0], (TOKENS, D), 1.0, 6.0, ((0, 32),)),
        "cotangent": bell_draw(keys[1], (TOKENS, D), 1.0, 6.0, ((0, 32),)),
        "route_experts": draw_route_experts(jax.random.fold_in(keys[7], 71), 0),
        "route_gates": jnp.clip(0.2 + 0.8 * jax.random.uniform(keys[3], (TOKENS, 2), jnp.float32) ** levels(keys[3], (TOKENS, 2), ((0, 8),), -0.2, 0.2), 0.2, 1.0),
        "w_gate": bell_draw(keys[4], (D, FF), D ** -0.5, 0.109375, ((0, 8), (1, 4))),
        "w_up": bell_draw(keys[5], (D, FF), D ** -0.5, 0.109375, ((0, 8), (1, 4))),
        "w_down": bell_draw(keys[6], (FF, D), FF ** -0.5, 0.0625, ((0, 4), (1, 8))),
    }


def route_table(route_experts, route_gates, slot_limit):
    is_first = route_experts[:, 0] == 0
    is_second = route_experts[:, 1] == 0
    chosen = jnp.logical_or(is_first, is_second)
    route_weight = jnp.where(is_first, route_gates[:, 0], 0.0) + jnp.where(is_second, route_gates[:, 1], 0.0)
    chosen_int = chosen.astype(jnp.int32)
    slot_of = (jnp.cumsum(chosen_int) - chosen_int).astype(jnp.int32)
    live_count = jnp.sum(chosen_int).astype(jnp.int32)
    target = jnp.where(chosen, slot_of, slot_limit).astype(jnp.int32)
    source = jnp.zeros((slot_limit,), jnp.int32).at[target].set(jnp.arange(route_experts.shape[0], dtype=jnp.int32), mode="drop")
    live_slot = jnp.arange(slot_limit, dtype=jnp.int32) < live_count
    return chosen, route_weight, jnp.where(chosen, slot_of, 0).astype(jnp.int32), source, live_slot


def group_pass(token_rows, upstream, route_experts, route_gates, w_gate, w_up, w_down):
    slot_limit = CAP
    chosen, route_weight, slot_of, source, live_slot = route_table(route_experts, route_gates, slot_limit)
    expert_rows = token_rows[source]
    gate_pre = jnp.dot(expert_rows, w_gate, preferred_element_type=jnp.float32)
    up_pre = jnp.dot(expert_rows, w_up, preferred_element_type=jnp.float32)
    gate_sig = jax.nn.sigmoid(gate_pre)
    hidden = (gate_pre * gate_sig * up_pre).astype(jnp.bfloat16)
    block_length = FF // N_ET
    hidden_state_blocks = hidden.astype(jnp.float32).reshape(slot_limit, N_ET, block_length)
    down_weight_blocks = w_down.astype(jnp.float32).reshape(N_ET, block_length, D)
    output_pieces = jnp.einsum("oku,kus->kos", hidden_state_blocks, down_weight_blocks).astype(jnp.bfloat16)
    out_sum = jnp.sum(output_pieces.astype(jnp.float32), axis=0)
    slot_weight = jnp.where(live_slot, route_weight[source], 0.0)
    slot_cot = (slot_weight[:, None] * upstream[source].astype(jnp.float32)).astype(jnp.bfloat16)
    grad_hidden = lax.dot_general(slot_cot, w_down, (((1,), (1,)), ((), ())), preferred_element_type=jnp.float32)
    gate_gradient = (grad_hidden * up_pre * gate_sig * (1.0 + gate_pre * (1.0 - gate_sig))).astype(jnp.bfloat16)
    up_gradient = (grad_hidden * gate_pre * gate_sig).astype(jnp.bfloat16)
    gate_weight_blocks = w_gate.astype(jnp.float32).reshape(D, N_ET, block_length)
    up_weight_blocks = w_up.astype(jnp.float32).reshape(D, N_ET, block_length)
    gradient_pieces = jnp.einsum("rjh,kjh->jrk", gate_gradient.astype(jnp.float32).reshape(slot_limit, N_ET, block_length), gate_weight_blocks)
    gradient_pieces = gradient_pieces + jnp.einsum("rjh,kjh->jrk", up_gradient.astype(jnp.float32).reshape(slot_limit, N_ET, block_length), up_weight_blocks)
    grad_sum = jnp.sum(gradient_pieces.astype(jnp.bfloat16).astype(jnp.float32), axis=0)
    moe_out = (route_weight[:, None] * out_sum[slot_of]).astype(jnp.bfloat16)
    grad_tokens = jnp.where(chosen[:, None], grad_sum[slot_of], 0.0).astype(jnp.bfloat16)
    return moe_out, grad_tokens


def reference(tokens, cotangent, route_experts, route_gates, w_gate, w_up, w_down):
    def by_group(values):
        return values.reshape((N_FSDP, values.shape[0] // N_FSDP) + values.shape[1:])

    def one_group(pieces):
        return group_pass(pieces[0], pieces[1], pieces[2], pieces[3], w_gate, w_up, w_down)

    moe_out, grad_tokens = lax.map(one_group, (by_group(tokens), by_group(cotangent), by_group(route_experts), by_group(route_gates)))
    return moe_out.reshape(tokens.shape), grad_tokens.reshape(tokens.shape)
```

```python
import jax
import jax.numpy as jnp
from jax import lax
from jax.sharding import PartitionSpec as P

F32 = jnp.float32
BF16 = jnp.bfloat16
PAIR = 2
CUTS = (0, 4, 8, 12, 14, 16)


def dot(left, right):
    return jnp.dot(left, right, preferred_element_type=F32)


def dot_last(left, right):
    return lax.dot_general(left, right, (((1,), (1,)), ((), ())), preferred_element_type=F32)


def make_per_device(n_fsdp, n_et):
    n_z = n_fsdp // PAIR
    half_z = n_z // 2

    def over_z(pairs):
        return [(a * PAIR + y, b * PAIR + y) for a, b in pairs for y in range(PAIR)]

    def z_swap(values, step):
        return lax.ppermute(values, "fsdp", over_z([(z, z ^ step) for z in range(n_z)]))

    def y_swap(values):
        return lax.ppermute(values, "fsdp", [(f, f ^ 1) for f in range(n_fsdp)])

    def e_swap(values, step):
        return lax.ppermute(values, "et", [(e, e ^ step) for e in range(n_et)])

    def inward(values, step):
        last = n_z - 1
        pairs = [(step, step + 1), (last - step, last - step - 1)]
        return lax.ppermute(values, "fsdp", over_z(pairs))

    def outward(values, step):
        last = n_z - 1
        pairs = [(step + 1, step), (last - step - 1, last - step)]
        return lax.ppermute(values, "fsdp", over_z(pairs))

    def middle_swap(values):
        return lax.ppermute(
            values, "fsdp", over_z([(half_z - 1, half_z), (half_z, half_z - 1)])
        )

    steps_e = []
    step = n_et // 2
    while step >= 1:
        steps_e.append(step)
        step //= 2

    def per_device(tokens, cotangent, route_experts, route_gates, w_gate, w_up, w_down):
        own_count, width = tokens.shape
        most = own_count // 8
        own_width, hidden_units = w_gate.shape
        z_width = own_width * PAIR
        f_index = lax.axis_index("fsdp")
        z_index = f_index // PAIR
        y_index = f_index % PAIR
        depth = jnp.minimum(z_index, n_z - 1 - z_index)

        cuts = [hidden_units * c // CUTS[-1] for c in CUTS]
        own_w, far_w = [], []
        for lo, hi in zip(cuts[:-1], cuts[1:]):
            own = (w_gate[:, lo:hi], w_up[:, lo:hi], w_down[lo:hi, :])
            own_w.append(own)
            far_w.append(tuple(y_swap(v) for v in own))

        own_start = lax.axis_index("et") * own_count
        own_experts = lax.dynamic_slice_in_dim(route_experts, own_start, own_count)
        own_gates = lax.dynamic_slice_in_dim(route_gates, own_start, own_count)
        is_first = own_experts[:, 0] == 0
        is_second = own_experts[:, 1] == 0
        chosen = jnp.logical_or(is_first, is_second)
        weight = jnp.where(is_first, own_gates[:, 0], 0.0) + jnp.where(
            is_second, own_gates[:, 1], 0.0
        )
        chosen_int = chosen.astype(jnp.int32)
        slot = jnp.cumsum(chosen_int) - chosen_int
        picks = jnp.logical_and(
            chosen[None, :], slot[None, :] == jnp.arange(most, dtype=jnp.int32)[:, None]
        )
        one_hot = picks.astype(BF16)
        packed_weight = jnp.sum(jnp.where(picks, weight[None, :], 0.0), axis=1)
        packed_rows = dot(one_hot, tokens).astype(BF16)
        packed_cot = (packed_weight[:, None] * dot(one_hot, cotangent)).astype(BF16)
        packed = jnp.concatenate([packed_rows, packed_cot], axis=0)

        pieces = []
        for d in range(n_z):
            start = (z_index ^ d) * z_width
            piece = lax.dynamic_slice_in_dim(packed, start, z_width, axis=1)
            pieces.append(piece if d == 0 else z_swap(piece, d))
        stacked = jnp.stack(pieces)
        order = jnp.arange(n_z, dtype=jnp.int32) ^ (z_index & (half_z - 1))
        stacked = jnp.take(stacked, order, axis=0)[None]
        for step in steps_e:
            stacked = jnp.concatenate([stacked, e_swap(stacked, step)], axis=0)
        stacked = jnp.swapaxes(stacked, 0, 1)
        slots = n_z * n_et * most
        rows = stacked[:, :, :most].reshape(slots, z_width)
        cots = stacked[:, :, most:].reshape(slots, z_width)
        own_at = y_index * own_width
        far_at = (PAIR - 1 - y_index) * own_width
        rows_own = lax.dynamic_slice_in_dim(rows, own_at, own_width, axis=1)
        rows_far = lax.dynamic_slice_in_dim(rows, far_at, own_width, axis=1)
        cots_own = lax.dynamic_slice_in_dim(cots, own_at, own_width, axis=1)
        cots_far = lax.dynamic_slice_in_dim(cots, far_at, own_width, axis=1)

        half = slots // 2
        total = None
        for own, far in zip(own_w, far_w):
            units = own[0].shape[1]
            gate = dot(rows_own, own[0]) + dot(rows_far, far[0])
            up = dot(rows_own, own[1]) + dot(rows_far, far[1])
            grad = dot_last(cots_own, own[2]) + dot_last(cots_far, far[2])
            part = jnp.concatenate([gate, up, grad], axis=1).astype(BF16)
            for step in range(half_z - 1):
                part = (part.astype(F32) + inward(part, step).astype(F32)).astype(BF16)
            pre = part[:half].astype(F32) + middle_swap(part[half:]).astype(F32)
            gate, up, grad = pre[:, :units], pre[:, units : 2 * units], pre[:, 2 * units :]
            sig = jax.nn.sigmoid(gate)
            hidden = gate * sig * up
            grad_gate = grad * up * sig * (1.0 + gate * (1.0 - sig))
            grad_up = grad * gate * sig
            near = jnp.concatenate([hidden, grad_gate, grad_up], axis=1).astype(BF16)
            other = middle_swap(near)
            for step in reversed(range(half_z - 1)):
                near = jnp.where(depth == step, outward(near, step), near)
                other = jnp.where(depth == step, outward(other, step), other)
            full = jnp.concatenate([near, other], axis=0)
            hidden, grad_gate, grad_up = (
                full[:, :units],
                full[:, units : 2 * units],
                full[:, 2 * units :],
            )
            terms = (
                dot(hidden, own[2]),
                dot(hidden, far[2]),
                dot_last(grad_gate, own[0]) + dot_last(grad_up, own[1]),
                dot_last(grad_gate, far[0]) + dot_last(grad_up, far[1]),
            )
            total = terms if total is None else tuple(a + b for a, b in zip(total, terms))

        is_low = y_index == 0
        both = []
        for own_part, far_part in ((total[0], total[1]), (total[2], total[3])):
            left = jnp.where(is_low, own_part, far_part)
            right = jnp.where(is_low, far_part, own_part)
            both.append(jnp.concatenate([left, right], axis=1))
        sums = jnp.stack(both).reshape(2, n_z, n_et, most, z_width)
        sums = jnp.transpose(sums, (2, 1, 0, 3, 4))
        for step in reversed(steps_e):
            count = sums.shape[0] // 2
            sums = sums[:count] + e_swap(sums[count:].astype(BF16), step).astype(F32)
        sums = sums[0].astype(BF16)
        sums = jnp.take(sums, order, axis=0)
        blocks = [sums[0]] + [z_swap(sums[d], d) for d in range(1, n_z)]
        blocks = jnp.take(jnp.stack(blocks), jnp.arange(n_z, dtype=jnp.int32) ^ z_index, axis=0)
        own_sums = jnp.transpose(blocks, (1, 2, 0, 3)).reshape(2, most, width)
        spread = one_hot.T
        moe_out = (weight[:, None] * dot(spread, own_sums[0])).astype(BF16)
        grad_tokens = dot(spread, own_sums[1]).astype(BF16)
        return moe_out, grad_tokens

    return per_device


def solution(mesh):
    sizes = dict(mesh.shape)
    in_specs = (
        P(("fsdp", "et"), None),
        P(("fsdp", "et"), None),
        P("fsdp", None),
        P("fsdp", None),
        P("fsdp", "et"),
        P("fsdp", "et"),
        P("et", "fsdp"),
    )
    out_specs = (P(("fsdp", "et"), None), P(("fsdp", "et"), None))
    return jax.shard_map(
        make_per_device(sizes["fsdp"], sizes["et"]),
        mesh=mesh,
        in_specs=in_specs,
        out_specs=out_specs,
        check_vma=False,
    )
```

```python
import jax
import jax.numpy as jnp
from jax import lax
from jax.experimental import pallas as pl
from jax.experimental.pallas import tpu as pltpu
from jax.sharding import PartitionSpec as P

F32 = jnp.float32
BF16 = jnp.bfloat16
LANES = 128
AHEAD = 2


def dot(left, right):
    return jnp.dot(left, right, preferred_element_type=F32)


def dot_last(left, right):
    return lax.dot_general(left, right, (((1,), (1,)), ((), ())), preferred_element_type=F32)


def chunk_cuts(units):
    blocks = units // LANES
    if blocks < 8:
        sizes = [1] * blocks
    else:
        sizes = [2 * (blocks // 8)] * 3 + [blocks // 8] * 2
    cuts = [0]
    for size in sizes:
        cuts.append(cuts[-1] + size * LANES)
    return cuts


def make_plain(n_fsdp, n_et):
    n_half = n_fsdp // 4

    def f_swap(values, mask):
        return lax.ppermute(values, "fsdp", [(f, f ^ mask) for f in range(n_fsdp)])

    def e_swap(values, mask):
        return lax.ppermute(values, "et", [(e, e ^ mask) for e in range(n_et)])

    def zp_flip(values):
        return jnp.concatenate([values[..., 1:2, :], values[..., 0:1, :]], axis=-2)

    def zp_step(values):
        return f_swap(zp_flip(values), 2)

    steps = [zp_step]
    mask = n_et // 2
    while mask >= 1:
        steps.append(lambda values, mask=mask: e_swap(values, mask))
        mask //= 2

    def per_device(tokens, cotangent, route_experts, route_gates, w_gate, w_up, w_down):
        own_count, width = tokens.shape
        most = own_count // 8
        own_width, hidden_units = w_gate.shape
        half_units = hidden_units // 2
        f_index = lax.axis_index("fsdp")
        z_half = f_index // 4
        z_low = (f_index // 2) % 2
        y_index = f_index % 2

        cuts = chunk_cuts(half_units)
        keep_at = z_low * half_units
        give_at = (1 - z_low) * half_units

        def part_of(start, size):
            return jnp.stack(
                [
                    lax.dynamic_slice_in_dim(w_gate, start, size, axis=1),
                    lax.dynamic_slice_in_dim(w_up, start, size, axis=1),
                    lax.dynamic_slice_in_dim(w_down, start, size, axis=0).T,
                ]
            )

        count = len(cuts) - 1
        kept, given = [], []
        for lo, hi in zip(cuts[:-1], cuts[1:]):
            kept.append(part_of(keep_at + lo, hi - lo))
            given.append(part_of(give_at + lo, hi - lo))
        near, far = [None] * count, [None] * count

        def start_pair(k):
            near[k] = jnp.concatenate([kept[k], f_swap(given[k], 2)], axis=1)

        first_far = f_swap(kept[0], 1)
        first_pair = f_swap(given[0], 2)
        near[0] = jnp.concatenate([kept[0], first_pair], axis=1)
        far[0] = jnp.concatenate([first_far, f_swap(first_pair, 1)], axis=1)
        for k in range(1, min(AHEAD, count)):
            start_pair(k)
            far[k] = f_swap(near[k], 1)

        own_start = lax.axis_index("et") * own_count
        own_experts = lax.dynamic_slice_in_dim(route_experts, own_start, own_count)
        own_gates = lax.dynamic_slice_in_dim(route_gates, own_start, own_count)
        is_first = own_experts[:, 0] == 0
        is_second = own_experts[:, 1] == 0
        chosen = jnp.logical_or(is_first, is_second)
        weight = jnp.where(is_first, own_gates[:, 0], 0.0) + jnp.where(
            is_second, own_gates[:, 1], 0.0
        )
        chosen_int = chosen.astype(jnp.int32)
        slot = jnp.cumsum(chosen_int) - chosen_int
        picks = jnp.logical_and(
            chosen[None, :], slot[None, :] == jnp.arange(most, dtype=jnp.int32)[:, None]
        )
        one_hot = picks.astype(BF16)
        packed_weight = jnp.sum(jnp.where(picks, weight[None, :], 0.0), axis=1)
        packed_rows = dot(one_hot, tokens).astype(BF16)
        packed_cot = (packed_weight[:, None] * dot(one_hot, cotangent)).astype(BF16)
        packed = jnp.concatenate([packed_rows, packed_cot], axis=0)

        cols = packed.reshape(2 * most, n_half, 2, 2, own_width)
        cols = jnp.where(z_low == 0, cols, cols[:, :, ::-1])
        cols = jnp.where(y_index == 0, cols, cols[:, :, :, ::-1])
        cols = jnp.transpose(cols, (1, 0, 3, 2, 4))
        blocks = []
        for d in range(n_half):
            block = lax.dynamic_index_in_dim(cols, z_half ^ d, 0, keepdims=False)
            blocks.append(block if d == 0 else f_swap(block, 4 * d))
        rows = jnp.stack(blocks)[None]
        for step in steps:
            rows = jnp.concatenate([rows, step(rows)], axis=0)
        members = rows.shape[0]
        slots = n_half * members * most
        rows = rows.reshape(members, n_half, 2, most, 2, 2 * own_width)
        rows = jnp.transpose(rows, (2, 4, 1, 0, 3, 5)).reshape(2, 2, slots, 2 * own_width)
        x_near, x_far, cot_near, cot_far = rows[0, 0], rows[0, 1], rows[1, 0], rows[1, 1]

        own_slots = slots // n_half
        total = None
        for k in range(count):
            units = kept[k].shape[2]
            near_k, far_k = near[k], far[k]
            gate = dot(x_near, near_k[0]) + dot(x_far, far_k[0])
            up = dot(x_near, near_k[1]) + dot(x_far, far_k[1])
            grad = dot(cot_near, near_k[2]) + dot(cot_far, far_k[2])
            part = jnp.concatenate([gate, up, grad], axis=1)
            sent = part[own_slots:].astype(BF16).reshape(n_half - 1, own_slots, 3 * units)
            if k + AHEAD < count:
                held = lax.optimization_barrier((kept[k + AHEAD], given[k + AHEAD], sent))
                kept[k + AHEAD], given[k + AHEAD], sent = held
                start_pair(k + AHEAD)
                far[k + AHEAD] = f_swap(near[k + AHEAD], 1)
            pre = part[:own_slots]
            for d in range(1, n_half):
                pre = pre + f_swap(sent[d - 1], 4 * d).astype(F32)
            gate, up, grad = pre[:, :units], pre[:, units : 2 * units], pre[:, 2 * units :]
            sig = jax.nn.sigmoid(gate)
            hidden = gate * sig * up
            grad_gate = grad * up * sig * (1.0 + gate * (1.0 - sig))
            grad_up = grad * gate * sig
            mine = jnp.concatenate([hidden, grad_gate, grad_up], axis=1).astype(BF16)
            full = jnp.concatenate([mine] + [f_swap(mine, 4 * d) for d in range(1, n_half)], axis=0)
            hidden, grad_gate, grad_up = (
                full[:, :units],
                full[:, units : 2 * units],
                full[:, 2 * units :],
            )
            terms = (
                dot_last(hidden, near_k[2]),
                dot_last(hidden, far_k[2]),
                dot_last(grad_gate, near_k[0]) + dot_last(grad_up, near_k[1]),
                dot_last(grad_gate, far_k[0]) + dot_last(grad_up, far_k[1]),
            )
            total = terms if total is None else tuple(a + b for a, b in zip(total, terms))

        sums = jnp.stack([jnp.stack(total[:2]), jnp.stack(total[2:])])
        sums = sums.reshape(2, 2, n_half, members, most, 2, own_width)
        sums = jnp.transpose(sums, (3, 2, 0, 4, 1, 5, 6))
        for step in reversed(steps):
            rest = sums.shape[0] // 2
            sums = sums[:rest] + step(sums[rest:].astype(BF16)).astype(F32)
        sums = sums[0].astype(BF16)
        back = [sums[0]] + [f_swap(sums[d], 4 * d) for d in range(1, n_half)]
        back = jnp.stack(back)
        order = jnp.arange(n_half, dtype=jnp.int32) ^ z_half
        back = jnp.take(back, order, axis=0)
        back = jnp.transpose(back, (1, 2, 0, 4, 3, 5))
        back = jnp.where(z_low == 0, back, back[:, :, :, ::-1])
        back = jnp.where(y_index == 0, back, back[:, :, :, :, ::-1])
        own_sums = back.reshape(2, most, width)
        spread = one_hot.T
        moe_out = (weight[:, None] * dot(spread, own_sums[0])).astype(BF16)
        grad_tokens = dot(spread, own_sums[1]).astype(BF16)
        return moe_out, grad_tokens

    return per_device


def call(body, outs, *args, scratch=(), flops=0):
    moved = sum(v.size * v.dtype.itemsize for v in list(args) + list(outs))
    return pl.pallas_call(
        body,
        out_shape=list(outs),
        scratch_shapes=list(scratch),
        compiler_params=pltpu.CompilerParams(vmem_limit_bytes=40 * 1024 * 1024),
        cost_estimate=pl.CostEstimate(flops=flops, bytes_accessed=moved, transcendentals=0),
    )(*args)


def shaped(shape, kind):
    return jax.ShapeDtypeStruct(shape, kind)


def flip_pairs(values, own_width):
    parts = [values[..., i * own_width : (i + 1) * own_width] for i in (1, 0, 3, 2)]
    return jnp.concatenate(parts, axis=-1)


def route_columns(experts_ref, gates_ref):
    count = experts_ref.shape[0] // 4
    start = pl.multiple_of(lax.axis_index("et") * count, count)
    experts = experts_ref[pl.ds(start, count), :]
    gates = gates_ref[pl.ds(start, count), :]
    hits = (experts == 0).astype(F32)
    chosen = jnp.sum(hits, axis=1, keepdims=True)
    weight = jnp.sum(hits * gates, axis=1, keepdims=True)
    return chosen, weight


def as_row(column, keep):
    return jnp.sum(jnp.where(keep, column, 0.0), axis=0, keepdims=True)


def weight_chunk_body(low_ref, *refs):
    for gate, up, down, out in (refs[0:3] + refs[6:7], refs[3:6] + refs[7:8]):
        out[0] = gate[...]
        out[1] = up[...]
        out[2] = down[...].T


def weight_chunk(low, w_gate, w_up, w_down, lo, size):
    own_width, hidden_units = w_gate.shape
    half = hidden_units // 2 // size
    at = lo // size

    def spec(kept, rows):
        def index(i, low_ref):
            block = at + half * (low_ref[0] if kept else 1 - low_ref[0])
            return (block, 0) if rows else (0, block)

        return pl.BlockSpec((size, own_width) if rows else (own_width, size), index)

    out = shaped((3, own_width, size), BF16)
    specs = [spec(kept, rows) for kept in (True, False) for rows in (False, False, True)]
    whole = pl.BlockSpec((3, own_width, size), lambda i, low_ref: (0, 0, 0))
    return pl.pallas_call(
        weight_chunk_body,
        out_shape=[out, out],
        grid_spec=pltpu.PrefetchScalarGridSpec(
            num_scalar_prefetch=1, grid=(1,), in_specs=specs, out_specs=[whole, whole]
        ),
        compiler_params=pltpu.CompilerParams(vmem_limit_bytes=40 * 1024 * 1024),
        cost_estimate=pl.CostEstimate(
            flops=0, bytes_accessed=12 * out.size * 2, transcendentals=0
        ),
    )(low, w_gate, w_up, w_down, w_gate, w_up, w_down)


def make_fused(n_fsdp, n_et):
    world = n_fsdp * n_et

    def swap(values, mask):
        pairs = [(i, i ^ mask) for i in range(world)]
        return lax.ppermute(values, ("fsdp", "et"), pairs)

    at_y, at_zp, at_zh = n_et, 2 * n_et, 4 * n_et
    at_core, at_x = 1, 2

    def per_device(tokens, cotangent, route_experts, route_gates, w_gate, w_up, w_down):
        own_count, width = tokens.shape
        most = own_count // 8
        own_width, hidden_units = w_gate.shape
        half_units = hidden_units // 2
        z_width = 4 * own_width
        block_shape = (2, most, z_width)
        low = ((lax.axis_index("fsdp") // 2) % 2).astype(jnp.int32).reshape(1)

        cuts = chunk_cuts(half_units)
        count = len(cuts) - 1
        own_w, zp_w, far_own, far_zp = ([None] * count for _ in range(4))
        given = [None] * count

        def make_chunk(k):
            own_w[k], given[k] = weight_chunk(
                low, w_gate, w_up, w_down, cuts[k], cuts[k + 1] - cuts[k]
            )

        def send_chunk(k):
            zp_w[k] = swap(given[k], at_zp)
            far_own[k] = swap(own_w[k], at_y)
            far_zp[k] = swap(zp_w[k], at_y)

        make_chunk(0)
        send_chunk(0)
        tokens, cotangent, own_w[0] = lax.optimization_barrier((tokens, cotangent, own_w[0]))

        def pack_body(tokens_ref, cot_ref, experts_ref, gates_ref, keep_ref, send_ref, packed_ref):
            chosen, weight = route_columns(experts_ref, gates_ref)
            shape = (own_count, own_count)
            down = lax.broadcasted_iota(jnp.int32, shape, 0)
            across = lax.broadcasted_iota(jnp.int32, shape, 1)
            chosen_row = as_row(chosen, down == across)
            weight_row = as_row(weight, down == across)
            slot_row = as_row(chosen, down < across)
            places = lax.broadcasted_iota(jnp.int32, (most, own_count), 0).astype(F32)
            picks = jnp.logical_and(slot_row == places, chosen_row > 0.0)
            one_hot = jnp.where(picks, 1.0, 0.0).astype(BF16)
            slot_weight = jnp.sum(jnp.where(picks, weight_row, 0.0), axis=1, keepdims=True)
            packed_ref[0] = dot(one_hot, tokens_ref[...]).astype(BF16)
            packed_ref[1] = (slot_weight * dot(one_hot, cot_ref[...])).astype(BF16)
            f_index = lax.axis_index("fsdp")
            for d, out in enumerate((keep_ref, send_ref)):
                for i in range(4):
                    mask = 4 * d + 2 * (i % 2) + i // 2
                    start = pl.multiple_of((f_index ^ mask) * own_width, LANES)
                    columns = slice(i * own_width, (i + 1) * own_width)
                    out[:, :, columns] = packed_ref[:, :, pl.ds(start, own_width)]

        block = shaped(block_shape, BF16)
        mine, sent = call(
            pack_body,
            [block, block],
            tokens,
            cotangent,
            route_experts,
            route_gates,
            scratch=[pltpu.VMEM((2, most, width), BF16)],
            flops=4 * most * own_count * width,
        )
        other = swap(sent, at_zh)
        if count > 1:
            make_chunk(1)
            send_chunk(1)

        def join_body(mine_ref, other_ref, plain_ref, flipped_ref):
            for j, ref in enumerate((mine_ref, other_ref)):
                values = ref[...]
                plain_ref[j] = values
                flipped_ref[j] = flip_pairs(values, own_width)

        pair = shaped((2,) + block_shape, BF16)
        plain, flipped = call(join_body, [pair, pair], mine, other)
        near_rows = jnp.stack(
            [plain, swap(plain, at_x), swap(flipped, at_zp), swap(flipped, at_zp + at_x)]
        )
        far_rows = swap(near_rows, at_core)

        slots = 16 * most
        own_slots = slots // 2

        def rows_of(near_ref, far_ref, which):
            parts = [ref[:, :, which].reshape(own_slots, z_width) for ref in (near_ref, far_ref)]
            return jnp.concatenate(parts, axis=0)

        def first_body(near_ref, far_ref, a_ref, b_ref, c_ref, d_ref, keep_ref, send_ref):
            units = a_ref.shape[2]
            rows = rows_of(near_ref, far_ref, 0)
            cots = rows_of(near_ref, far_ref, 1)
            for j in range(3):
                left = cots if j == 2 else rows
                value = None
                for i, ref in enumerate((a_ref, b_ref, c_ref, d_ref)):
                    term = dot(left[:, i * own_width : (i + 1) * own_width], ref[j])
                    value = term if value is None else value + term
                value = value.reshape(8, 2, most, units)
                columns = slice(j * units, (j + 1) * units)
                keep_ref[:, columns] = value[:, 0].reshape(own_slots, units)
                send_ref[:, columns] = value[:, 1].reshape(own_slots, units).astype(BF16)

        def middle_body(keep_ref, recv_ref, out_ref):
            units = keep_ref.shape[1] // 3
            pre = keep_ref[...] + recv_ref[...].astype(F32)
            gate, up, grad = pre[:, :units], pre[:, units : 2 * units], pre[:, 2 * units :]
            sig = 1.0 / (1.0 + jnp.exp(-gate))
            out_ref[:, :units] = (gate * sig * up).astype(BF16)
            out_ref[:, units : 2 * units] = (
                grad * up * sig * (1.0 + gate * (1.0 - sig))
            ).astype(BF16)
            out_ref[:, 2 * units :] = (grad * gate * sig).astype(BF16)

        def second_terms(mine_ref, recv_ref, refs):
            units = refs[0].shape[2]
            full = jnp.concatenate([mine_ref[...], recv_ref[...]], axis=0)
            hidden, grad_gate, grad_up = (
                full[:, j * units : (j + 1) * units] for j in range(3)
            )
            outs = [dot_last(hidden, ref[2]) for ref in refs]
            grads = [dot_last(grad_gate, ref[0]) + dot_last(grad_up, ref[1]) for ref in refs]
            return outs, grads

        def second_body(first, last, mine_ref, recv_ref, a_ref, b_ref, c_ref, d_ref, *rest):
            terms = second_terms(mine_ref, recv_ref, (a_ref, b_ref, c_ref, d_ref))
            rest = list(rest)
            held = None if first else rest.pop(0)
            for which in range(2):
                for i in range(4):
                    columns = slice(i * own_width, (i + 1) * own_width)
                    value = terms[which][i]
                    if held is not None:
                        value = value + held[which, :, columns]
                    if not last:
                        rest[0][which, :, columns] = value
                        continue
                    value = value.reshape(2, 2, 4, most, own_width)
                    for j in range(2):
                        rest[0][:, j, which, :, columns] = value[j, 0]
                        rest[1][:, j, which, :, columns] = value[j, 1].astype(BF16)

        total = None
        quad = (4, 2) + block_shape
        for k in range(count):
            units = cuts[k + 1] - cuts[k]
            work = 2 * slots * z_width * units * 3
            weights = (own_w[k], zp_w[k], far_own[k], far_zp[k])
            keep, sent = call(
                first_body,
                [shaped((own_slots, 3 * units), F32), shaped((own_slots, 3 * units), BF16)],
                near_rows,
                far_rows,
                *weights,
                flops=work,
            )
            if k + AHEAD < count:
                make_chunk(k + AHEAD)
                own_w[k + AHEAD], given[k + AHEAD], sent = lax.optimization_barrier(
                    (own_w[k + AHEAD], given[k + AHEAD], sent)
                )
                send_chunk(k + AHEAD)
            (mine,) = call(
                middle_body,
                [shaped((own_slots, 3 * units), BF16)],
                keep,
                swap(sent, at_zh),
            )
            first, last = k == 0, k == count - 1
            outs = (
                [shaped(quad, F32), shaped(quad, BF16)]
                if last
                else [shaped((2, slots, z_width), F32)]
            )
            held = () if first else (total,)
            total = call(
                lambda *refs, first=first, last=last: second_body(first, last, *refs),
                outs,
                mine,
                swap(mine, at_zh),
                *weights,
                *held,
                flops=work,
            )
            if not last:
                (total,) = total

        def spread_body(keep_ref, recv_ref, own_ref, *outs):
            value = keep_ref[...] + recv_ref[...].astype(F32)
            own_ref[...] = value[0]
            for i in range(1, 4):
                part = value[i].astype(BF16)
                outs[i - 1][...] = flip_pairs(part, own_width) if i >= 2 else part

        keep, sent = total
        own, by_x, by_zp, by_both = call(
            spread_body,
            [shaped(pair.shape, F32), pair, pair, pair],
            keep,
            swap(sent, at_core),
        )

        def gather_body(own_ref, x_ref, zp_ref, both_ref, keep_ref, send_ref):
            value = own_ref[...] + x_ref[...].astype(F32)
            value = value + (zp_ref[...].astype(F32) + both_ref[...].astype(F32))
            keep_ref[...] = value[0].astype(BF16)
            send_ref[...] = value[1].astype(BF16)

        mine, sent = call(
            gather_body,
            [block, block],
            own,
            swap(by_x, at_x),
            swap(by_zp, at_zp),
            swap(by_both, at_zp + at_x),
        )

        def unpack_body(mine_ref, other_ref, experts_ref, gates_ref, out_ref, grad_ref, sums_ref):
            f_index = lax.axis_index("fsdp")
            for d, ref in enumerate((mine_ref, other_ref)):
                for i in range(4):
                    mask = 4 * d + 2 * (i % 2) + i // 2
                    start = pl.multiple_of((f_index ^ mask) * own_width, LANES)
                    columns = slice(i * own_width, (i + 1) * own_width)
                    sums_ref[:, :, pl.ds(start, own_width)] = ref[:, :, columns]
            chosen, weight = route_columns(experts_ref, gates_ref)
            shape = (own_count, own_count)
            down = lax.broadcasted_iota(jnp.int32, shape, 0)
            across = lax.broadcasted_iota(jnp.int32, shape, 1)
            chosen_row = as_row(chosen, down == across)
            slot = jnp.sum(jnp.where(across < down, chosen_row, 0.0), axis=1, keepdims=True)
            places = lax.broadcasted_iota(jnp.int32, (own_count, most), 1).astype(F32)
            picks = jnp.logical_and(slot == places, chosen > 0.0)
            spread = jnp.where(picks, 1.0, 0.0).astype(BF16)
            out_ref[...] = (weight * dot(spread, sums_ref[0])).astype(BF16)
            grad_ref[...] = dot(spread, sums_ref[1]).astype(BF16)

        result = shaped(tokens.shape, BF16)
        return tuple(
            call(
                unpack_body,
                [result, result],
                mine,
                swap(sent, at_zh),
                route_experts,
                route_gates,
                scratch=[pltpu.VMEM((2, most, width), BF16)],
                flops=4 * most * own_count * width,
            )
        )

    return per_device


def solution(mesh):
    sizes = dict(mesh.shape)
    make = make_fused if sizes["fsdp"] == 8 and sizes["et"] == 4 else make_plain
    in_specs = (
        P(("fsdp", "et"), None),
        P(("fsdp", "et"), None),
        P("fsdp", None),
        P("fsdp", None),
        P("fsdp", "et"),
        P("fsdp", "et"),
        P("et", "fsdp"),
    )
    out_specs = (P(("fsdp", "et"), None), P(("fsdp", "et"), None))
    return jax.shard_map(
        make(sizes["fsdp"], sizes["et"]),
        mesh=mesh,
        in_specs=in_specs,
        out_specs=out_specs,
        check_vma=False,
    )
```

```python
import jax
import jax.numpy as jnp
from jax import lax
from jax.experimental import pallas as pl
from jax.experimental.pallas import tpu as pltpu
from jax.sharding import PartitionSpec as P

F32 = jnp.float32
BF16 = jnp.bfloat16
LANES = 128
AHEAD = 2
IN_FLIGHT = 2


def dot(left, right):
    return jnp.dot(left, right, preferred_element_type=F32)


def dot_last(left, right):
    return lax.dot_general(left, right, (((1,), (1,)), ((), ())), preferred_element_type=F32)


def chunk_cuts(units):
    blocks = units // LANES
    if blocks < 8:
        sizes = [1] * blocks
    else:
        sizes = [2 * (blocks // 8)] * 3 + [blocks // 8] * 2
    cuts = [0]
    for size in sizes:
        cuts.append(cuts[-1] + size * LANES)
    return cuts


def make_plain(n_fsdp, n_et):
    n_half = n_fsdp // 4

    def f_swap(values, mask):
        return lax.ppermute(values, "fsdp", [(f, f ^ mask) for f in range(n_fsdp)])

    def e_swap(values, mask):
        return lax.ppermute(values, "et", [(e, e ^ mask) for e in range(n_et)])

    def zp_flip(values):
        return jnp.concatenate([values[..., 1:2, :], values[..., 0:1, :]], axis=-2)

    def zp_step(values):
        return f_swap(zp_flip(values), 2)

    steps = [zp_step]
    mask = n_et // 2
    while mask >= 1:
        steps.append(lambda values, mask=mask: e_swap(values, mask))
        mask //= 2

    def per_device(tokens, cotangent, route_experts, route_gates, w_gate, w_up, w_down):
        own_count, width = tokens.shape
        most = own_count // 8
        own_width, hidden_units = w_gate.shape
        half_units = hidden_units // 2
        f_index = lax.axis_index("fsdp")
        z_half = f_index // 4
        z_low = (f_index // 2) % 2
        y_index = f_index % 2

        cuts = chunk_cuts(half_units)
        keep_at = z_low * half_units
        give_at = (1 - z_low) * half_units

        def part_of(start, size):
            return jnp.stack(
                [
                    lax.dynamic_slice_in_dim(w_gate, start, size, axis=1),
                    lax.dynamic_slice_in_dim(w_up, start, size, axis=1),
                    lax.dynamic_slice_in_dim(w_down, start, size, axis=0).T,
                ]
            )

        count = len(cuts) - 1
        kept, given = [], []
        for lo, hi in zip(cuts[:-1], cuts[1:]):
            kept.append(part_of(keep_at + lo, hi - lo))
            given.append(part_of(give_at + lo, hi - lo))
        near, far = [None] * count, [None] * count

        def start_pair(k):
            near[k] = jnp.concatenate([kept[k], f_swap(given[k], 2)], axis=1)

        first_far = f_swap(kept[0], 1)
        first_pair = f_swap(given[0], 2)
        near[0] = jnp.concatenate([kept[0], first_pair], axis=1)
        far[0] = jnp.concatenate([first_far, f_swap(first_pair, 1)], axis=1)
        for k in range(1, min(AHEAD, count)):
            start_pair(k)
            far[k] = f_swap(near[k], 1)

        own_start = lax.axis_index("et") * own_count
        own_experts = lax.dynamic_slice_in_dim(route_experts, own_start, own_count)
        own_gates = lax.dynamic_slice_in_dim(route_gates, own_start, own_count)
        is_first = own_experts[:, 0] == 0
        is_second = own_experts[:, 1] == 0
        chosen = jnp.logical_or(is_first, is_second)
        weight = jnp.where(is_first, own_gates[:, 0], 0.0) + jnp.where(
            is_second, own_gates[:, 1], 0.0
        )
        chosen_int = chosen.astype(jnp.int32)
        slot = jnp.cumsum(chosen_int) - chosen_int
        picks = jnp.logical_and(
            chosen[None, :], slot[None, :] == jnp.arange(most, dtype=jnp.int32)[:, None]
        )
        one_hot = picks.astype(BF16)
        packed_weight = jnp.sum(jnp.where(picks, weight[None, :], 0.0), axis=1)
        packed_rows = dot(one_hot, tokens).astype(BF16)
        packed_cot = (packed_weight[:, None] * dot(one_hot, cotangent)).astype(BF16)
        packed = jnp.concatenate([packed_rows, packed_cot], axis=0)

        cols = packed.reshape(2 * most, n_half, 2, 2, own_width)
        cols = jnp.where(z_low == 0, cols, cols[:, :, ::-1])
        cols = jnp.where(y_index == 0, cols, cols[:, :, :, ::-1])
        cols = jnp.transpose(cols, (1, 0, 3, 2, 4))
        blocks = []
        for d in range(n_half):
            block = lax.dynamic_index_in_dim(cols, z_half ^ d, 0, keepdims=False)
            blocks.append(block if d == 0 else f_swap(block, 4 * d))
        rows = jnp.stack(blocks)[None]
        for step in steps:
            rows = jnp.concatenate([rows, step(rows)], axis=0)
        members = rows.shape[0]
        slots = n_half * members * most
        rows = rows.reshape(members, n_half, 2, most, 2, 2 * own_width)
        rows = jnp.transpose(rows, (2, 4, 1, 0, 3, 5)).reshape(2, 2, slots, 2 * own_width)
        x_near, x_far, cot_near, cot_far = rows[0, 0], rows[0, 1], rows[1, 0], rows[1, 1]

        own_slots = slots // n_half
        total = None
        for k in range(count):
            units = kept[k].shape[2]
            near_k, far_k = near[k], far[k]
            gate = dot(x_near, near_k[0]) + dot(x_far, far_k[0])
            up = dot(x_near, near_k[1]) + dot(x_far, far_k[1])
            grad = dot(cot_near, near_k[2]) + dot(cot_far, far_k[2])
            part = jnp.concatenate([gate, up, grad], axis=1)
            sent = part[own_slots:].astype(BF16).reshape(n_half - 1, own_slots, 3 * units)
            if k + AHEAD < count:
                held = lax.optimization_barrier((kept[k + AHEAD], given[k + AHEAD], sent))
                kept[k + AHEAD], given[k + AHEAD], sent = held
                start_pair(k + AHEAD)
                far[k + AHEAD] = f_swap(near[k + AHEAD], 1)
            pre = part[:own_slots]
            for d in range(1, n_half):
                pre = pre + f_swap(sent[d - 1], 4 * d).astype(F32)
            gate, up, grad = pre[:, :units], pre[:, units : 2 * units], pre[:, 2 * units :]
            sig = jax.nn.sigmoid(gate)
            hidden = gate * sig * up
            grad_gate = grad * up * sig * (1.0 + gate * (1.0 - sig))
            grad_up = grad * gate * sig
            mine = jnp.concatenate([hidden, grad_gate, grad_up], axis=1).astype(BF16)
            full = jnp.concatenate([mine] + [f_swap(mine, 4 * d) for d in range(1, n_half)], axis=0)
            hidden, grad_gate, grad_up = (
                full[:, :units],
                full[:, units : 2 * units],
                full[:, 2 * units :],
            )
            terms = (
                dot_last(hidden, near_k[2]),
                dot_last(hidden, far_k[2]),
                dot_last(grad_gate, near_k[0]) + dot_last(grad_up, near_k[1]),
                dot_last(grad_gate, far_k[0]) + dot_last(grad_up, far_k[1]),
            )
            total = terms if total is None else tuple(a + b for a, b in zip(total, terms))

        sums = jnp.stack([jnp.stack(total[:2]), jnp.stack(total[2:])])
        sums = sums.reshape(2, 2, n_half, members, most, 2, own_width)
        sums = jnp.transpose(sums, (3, 2, 0, 4, 1, 5, 6))
        for step in reversed(steps):
            rest = sums.shape[0] // 2
            sums = sums[:rest] + step(sums[rest:].astype(BF16)).astype(F32)
        sums = sums[0].astype(BF16)
        back = [sums[0]] + [f_swap(sums[d], 4 * d) for d in range(1, n_half)]
        back = jnp.stack(back)
        order = jnp.arange(n_half, dtype=jnp.int32) ^ z_half
        back = jnp.take(back, order, axis=0)
        back = jnp.transpose(back, (1, 2, 0, 4, 3, 5))
        back = jnp.where(z_low == 0, back, back[:, :, :, ::-1])
        back = jnp.where(y_index == 0, back, back[:, :, :, :, ::-1])
        own_sums = back.reshape(2, most, width)
        spread = one_hot.T
        moe_out = (weight[:, None] * dot(spread, own_sums[0])).astype(BF16)
        grad_tokens = dot(spread, own_sums[1]).astype(BF16)
        return moe_out, grad_tokens

    return per_device


def call(body, outs, *args, scratch=(), flops=0):
    moved = sum(v.size * v.dtype.itemsize for v in list(args) + list(outs))
    return pl.pallas_call(
        body,
        out_shape=list(outs),
        scratch_shapes=list(scratch),
        compiler_params=pltpu.CompilerParams(vmem_limit_bytes=40 * 1024 * 1024),
        cost_estimate=pl.CostEstimate(flops=0, bytes_accessed=1024, transcendentals=0),
    )(*args)


def shaped(shape, kind):
    return jax.ShapeDtypeStruct(shape, kind)


def flip_pairs(values, own_width):
    parts = [values[..., i * own_width : (i + 1) * own_width] for i in (1, 0, 3, 2)]
    return jnp.concatenate(parts, axis=-1)


def route_columns(experts_ref, gates_ref):
    count = experts_ref.shape[0] // 4
    start = pl.multiple_of(lax.axis_index("et") * count, count)
    experts = experts_ref[pl.ds(start, count), :]
    gates = gates_ref[pl.ds(start, count), :]
    hits = (experts == 0).astype(F32)
    chosen = jnp.sum(hits, axis=1, keepdims=True)
    weight = jnp.sum(hits * gates, axis=1, keepdims=True)
    return chosen, weight


def as_row(column, keep):
    return jnp.sum(jnp.where(keep, column, 0.0), axis=0, keepdims=True)


def weight_chunk_body(low_ref, *refs):
    for gate, up, down, out in (refs[0:3] + refs[6:7], refs[3:6] + refs[7:8]):
        out[0] = gate[...]
        out[1] = up[...]
        out[2] = down[...].T


def weight_chunk(low, w_gate, w_up, w_down, lo, size):
    own_width, hidden_units = w_gate.shape
    half = hidden_units // 2 // size
    at = lo // size

    def spec(kept, rows):
        def index(i, low_ref):
            block = at + half * (low_ref[0] if kept else 1 - low_ref[0])
            return (block, 0) if rows else (0, block)

        return pl.BlockSpec((size, own_width) if rows else (own_width, size), index)

    out = shaped((3, own_width, size), BF16)
    specs = [spec(kept, rows) for kept in (True, False) for rows in (False, False, True)]
    whole = pl.BlockSpec((3, own_width, size), lambda i, low_ref: (0, 0, 0))
    return pl.pallas_call(
        weight_chunk_body,
        out_shape=[out, out],
        grid_spec=pltpu.PrefetchScalarGridSpec(
            num_scalar_prefetch=1, grid=(1,), in_specs=specs, out_specs=[whole, whole]
        ),
        compiler_params=pltpu.CompilerParams(vmem_limit_bytes=60 * 1024 * 1024),
        cost_estimate=pl.CostEstimate(
            flops=0, bytes_accessed=1024, transcendentals=0
        ),
    )(low, w_gate, w_up, w_down, w_gate, w_up, w_down)


def make_fused(n_fsdp, n_et):
    world = n_fsdp * n_et

    def swap(values, mask):
        pairs = [(i, i ^ mask) for i in range(world)]
        return lax.ppermute(values, ("fsdp", "et"), pairs)

    at_y, at_zp, at_zh = n_et, 2 * n_et, 4 * n_et
    at_core, at_x = 1, 2

    def per_device(tokens, cotangent, route_experts, route_gates, w_gate, w_up, w_down):
        own_count, width = tokens.shape
        most = own_count // 8
        own_width, hidden_units = w_gate.shape
        half_units = hidden_units // 2
        z_width = 4 * own_width
        block_shape = (2, most, z_width)
        low = ((lax.axis_index("fsdp") // 2) % 2).astype(jnp.int32).reshape(1)

        cuts = chunk_cuts(half_units)
        count = len(cuts) - 1
        own_w, zp_w = [None] * count, [None] * count
        given = [None] * count

        stream = []

        def over_y(values, *after):
            after = list(after)
            if len(stream) >= IN_FLIGHT:
                after.append(stream[-IN_FLIGHT])
            if after:
                values, *after = lax.optimization_barrier((values, *after))
            if len(stream) >= IN_FLIGHT:
                stream[-IN_FLIGHT] = after.pop()
            stream.append(swap(values, at_y))
            return after

        def stream_chunk(k, *after):
            own_w[k], given[k] = weight_chunk(
                low, w_gate, w_up, w_down, cuts[k], cuts[k + 1] - cuts[k]
            )
            zp_w[k] = swap(given[k], at_zp)
            after = over_y(own_w[k], *after)
            over_y(zp_w[k])
            return after

        for k in range(min(AHEAD, count)):
            stream_chunk(k)

        def pack_body(tokens_ref, cot_ref, experts_ref, gates_ref, keep_ref, send_ref, packed_ref):
            chosen, weight = route_columns(experts_ref, gates_ref)
            shape = (own_count, own_count)
            down = lax.broadcasted_iota(jnp.int32, shape, 0)
            across = lax.broadcasted_iota(jnp.int32, shape, 1)
            chosen_row = as_row(chosen, down == across)
            weight_row = as_row(weight, down == across)
            slot_row = as_row(chosen, down < across)
            places = lax.broadcasted_iota(jnp.int32, (most, own_count), 0).astype(F32)
            picks = jnp.logical_and(slot_row == places, chosen_row > 0.0)
            one_hot = jnp.where(picks, 1.0, 0.0).astype(BF16)
            slot_weight = jnp.sum(jnp.where(picks, weight_row, 0.0), axis=1, keepdims=True)
            packed_ref[0] = dot(one_hot, tokens_ref[...]).astype(BF16)
            packed_ref[1] = (slot_weight * dot(one_hot, cot_ref[...])).astype(BF16)
            f_index = lax.axis_index("fsdp")
            for d, out in enumerate((keep_ref, send_ref)):
                for i in range(4):
                    mask = 4 * d + 2 * (i % 2) + i // 2
                    start = pl.multiple_of((f_index ^ mask) * own_width, LANES)
                    columns = slice(i * own_width, (i + 1) * own_width)
                    out[:, :, columns] = packed_ref[:, :, pl.ds(start, own_width)]

        block = shaped(block_shape, BF16)
        mine, sent = call(
            pack_body,
            [block, block],
            tokens,
            cotangent,
            route_experts,
            route_gates,
            scratch=[pltpu.VMEM((2, most, width), BF16)],
            flops=4 * most * own_count * width,
        )
        other = swap(sent, at_zh)

        def join_body(mine_ref, other_ref, plain_ref, flipped_ref):
            for j, ref in enumerate((mine_ref, other_ref)):
                values = ref[...]
                plain_ref[j] = values
                flipped_ref[j] = flip_pairs(values, own_width)

        pair = shaped((2,) + block_shape, BF16)
        plain, flipped = call(join_body, [pair, pair], mine, other)
        near_rows = jnp.stack(
            [plain, swap(plain, at_x), swap(flipped, at_zp), swap(flipped, at_zp + at_x)]
        )
        far_rows = swap(near_rows, at_core)

        slots = 16 * most
        own_slots = slots // 2

        def rows_of(near_ref, far_ref, which):
            parts = [ref[:, :, which].reshape(own_slots, z_width) for ref in (near_ref, far_ref)]
            return jnp.concatenate(parts, axis=0)

        def first_body(near_ref, far_ref, a_ref, b_ref, c_ref, d_ref, keep_ref, send_ref):
            units = a_ref.shape[2]
            rows = rows_of(near_ref, far_ref, 0)
            cots = rows_of(near_ref, far_ref, 1)
            for j in range(3):
                left = cots if j == 2 else rows
                value = None
                for i, ref in enumerate((a_ref, b_ref, c_ref, d_ref)):
                    term = dot(left[:, i * own_width : (i + 1) * own_width], ref[j])
                    value = term if value is None else value + term
                value = value.reshape(8, 2, most, units)
                columns = slice(j * units, (j + 1) * units)
                keep_ref[:, columns] = value[:, 0].reshape(own_slots, units)
                send_ref[:, columns] = value[:, 1].reshape(own_slots, units).astype(BF16)

        def middle_body(keep_ref, recv_ref, out_ref):
            units = keep_ref.shape[1] // 3
            pre = keep_ref[...] + recv_ref[...].astype(F32)
            gate, up, grad = pre[:, :units], pre[:, units : 2 * units], pre[:, 2 * units :]
            sig = 1.0 / (1.0 + jnp.exp(-gate))
            out_ref[:, :units] = (gate * sig * up).astype(BF16)
            out_ref[:, units : 2 * units] = (
                grad * up * sig * (1.0 + gate * (1.0 - sig))
            ).astype(BF16)
            out_ref[:, 2 * units :] = (grad * gate * sig).astype(BF16)

        def second_terms(mine_ref, recv_ref, refs):
            units = refs[0].shape[2]
            full = jnp.concatenate([mine_ref[...], recv_ref[...]], axis=0)
            hidden, grad_gate, grad_up = (
                full[:, j * units : (j + 1) * units] for j in range(3)
            )
            outs = [dot_last(hidden, ref[2]) for ref in refs]
            grads = [dot_last(grad_gate, ref[0]) + dot_last(grad_up, ref[1]) for ref in refs]
            return outs, grads

        def second_body(first, last, mine_ref, recv_ref, a_ref, b_ref, c_ref, d_ref, *rest):
            terms = second_terms(mine_ref, recv_ref, (a_ref, b_ref, c_ref, d_ref))
            rest = list(rest)
            held = None if first else rest.pop(0)
            for which in range(2):
                for i in range(4):
                    columns = slice(i * own_width, (i + 1) * own_width)
                    value = terms[which][i]
                    if held is not None:
                        value = value + held[which, :, columns]
                    if not last:
                        rest[0][which, :, columns] = value
                        continue
                    value = value.reshape(2, 2, 4, most, own_width)
                    for j in range(2):
                        rest[0][:, j, which, :, columns] = value[j, 0]
                        rest[1][:, j, which, :, columns] = value[j, 1].astype(BF16)

        quad = (4, 2) + block_shape
        pre, mine, total = [None] * count, [None] * count, [None] * count

        def weights_of(k):
            return own_w[k], zp_w[k], stream[2 * k], stream[2 * k + 1]

        def first(k, near_rows, far_rows):
            units = cuts[k + 1] - cuts[k]
            pre[k] = call(
                first_body,
                [shaped((own_slots, 3 * units), F32), shaped((own_slots, 3 * units), BF16)],
                near_rows,
                far_rows,
                *weights_of(k),
            )

        def middle(k):
            units = cuts[k + 1] - cuts[k]
            keep, sent = pre[k]
            (mine[k],) = call(
                middle_body,
                [shaped((own_slots, 3 * units), BF16)],
                keep,
                swap(sent, at_zh),
            )

        def second(k):
            is_first, is_last = k == 0, k == count - 1
            outs = (
                [shaped(quad, F32), shaped(quad, BF16)]
                if is_last
                else [shaped((2, slots, z_width), F32)]
            )
            held = () if is_first else total[k - 1]
            total[k] = call(
                lambda *refs: second_body(is_first, is_last, *refs),
                outs,
                mine[k],
                swap(mine[k], at_zh),
                *weights_of(k),
                *held,
            )

        for k in range(count):
            if k == count - 1:
                after = [near_rows]
                if k >= 1:
                    after.append(mine[k - 1])
                if k >= 2:
                    after.append(total[k - 2][0])
                after = lax.optimization_barrier(tuple(after))
                near_rows = after[0]
                if k >= 1:
                    mine[k - 1] = after[1]
                if k >= 2:
                    total[k - 2] = [after[2]]
            first(k, near_rows, far_rows)
            if k + AHEAD < count:
                after = [pre[k][1]]
                if k >= 1:
                    after.append(mine[k - 1])
                if k >= 2:
                    after.append(total[k - 2][0])
                after = stream_chunk(k + AHEAD, *after)
                pre[k] = [pre[k][0], after[0]]
                if k >= 1:
                    mine[k - 1] = after[1]
                if k >= 2:
                    total[k - 2] = [after[2]]
            middle(k)
            if k >= 1:
                second(k - 1)
        second(count - 1)
        total = total[-1]

        def spread_body(keep_ref, recv_ref, own_ref, *outs):
            value = keep_ref[...] + recv_ref[...].astype(F32)
            own_ref[...] = value[0]
            for i in range(1, 4):
                part = value[i].astype(BF16)
                outs[i - 1][...] = flip_pairs(part, own_width) if i >= 2 else part

        keep, sent = total
        own, by_x, by_zp, by_both = call(
            spread_body,
            [shaped(pair.shape, F32), pair, pair, pair],
            keep,
            swap(sent, at_core),
        )

        def gather_body(own_ref, x_ref, zp_ref, both_ref, keep_ref, send_ref):
            value = own_ref[...] + x_ref[...].astype(F32)
            value = value + (zp_ref[...].astype(F32) + both_ref[...].astype(F32))
            keep_ref[...] = value[0].astype(BF16)
            send_ref[...] = value[1].astype(BF16)

        mine, sent = call(
            gather_body,
            [block, block],
            own,
            swap(by_x, at_x),
            swap(by_zp, at_zp),
            swap(by_both, at_zp + at_x),
        )

        def unpack_body(mine_ref, other_ref, experts_ref, gates_ref, out_ref, grad_ref, sums_ref):
            f_index = lax.axis_index("fsdp")
            for d, ref in enumerate((mine_ref, other_ref)):
                for i in range(4):
                    mask = 4 * d + 2 * (i % 2) + i // 2
                    start = pl.multiple_of((f_index ^ mask) * own_width, LANES)
                    columns = slice(i * own_width, (i + 1) * own_width)
                    sums_ref[:, :, pl.ds(start, own_width)] = ref[:, :, columns]
            chosen, weight = route_columns(experts_ref, gates_ref)
            shape = (own_count, own_count)
            down = lax.broadcasted_iota(jnp.int32, shape, 0)
            across = lax.broadcasted_iota(jnp.int32, shape, 1)
            chosen_row = as_row(chosen, down == across)
            slot = jnp.sum(jnp.where(across < down, chosen_row, 0.0), axis=1, keepdims=True)
            places = lax.broadcasted_iota(jnp.int32, (own_count, most), 1).astype(F32)
            picks = jnp.logical_and(slot == places, chosen > 0.0)
            spread = jnp.where(picks, 1.0, 0.0).astype(BF16)
            out_ref[...] = (weight * dot(spread, sums_ref[0])).astype(BF16)
            grad_ref[...] = dot(spread, sums_ref[1]).astype(BF16)

        result = shaped(tokens.shape, BF16)
        return tuple(
            call(
                unpack_body,
                [result, result],
                mine,
                swap(sent, at_zh),
                route_experts,
                route_gates,
                scratch=[pltpu.VMEM((2, most, width), BF16)],
                flops=4 * most * own_count * width,
            )
        )

    return per_device


def solution(mesh):
    sizes = dict(mesh.shape)
    make = make_fused if sizes["fsdp"] == 8 and sizes["et"] == 4 else make_plain
    in_specs = (
        P(("fsdp", "et"), None),
        P(("fsdp", "et"), None),
        P("fsdp", None),
        P("fsdp", None),
        P("fsdp", "et"),
        P("fsdp", "et"),
        P("et", "fsdp"),
    )
    out_specs = (P(("fsdp", "et"), None), P(("fsdp", "et"), None))
    return jax.shard_map(
        make(sizes["fsdp"], sizes["et"]),
        mesh=mesh,
        in_specs=in_specs,
        out_specs=out_specs,
        check_vma=False,
    )
```

```python
import jax
import jax.numpy as jnp
from jax import lax
from jax.experimental import pallas as pl
from jax.experimental.pallas import tpu as pltpu
from jax.sharding import PartitionSpec as P

F32 = jnp.float32
BF16 = jnp.bfloat16
LANES = 128
AHEAD = 2


def dot(left, right):
    return jnp.dot(left, right, preferred_element_type=F32)


def dot_last(left, right):
    return lax.dot_general(left, right, (((1,), (1,)), ((), ())), preferred_element_type=F32)


def chunk_list(units):
    blocks = units // LANES
    if blocks != 8:
        return [(i * LANES, LANES) for i in range(blocks)]
    shape = ((0, 1), (2, 2), (4, 2), (6, 2), (1, 1))
    return [(start * LANES, size * LANES) for start, size in shape]


def make_plain(n_fsdp, n_et):
    n_half = n_fsdp // 4

    def f_swap(values, mask):
        return lax.ppermute(values, "fsdp", [(f, f ^ mask) for f in range(n_fsdp)])

    def e_swap(values, mask):
        return lax.ppermute(values, "et", [(e, e ^ mask) for e in range(n_et)])

    def zp_flip(values):
        return jnp.concatenate([values[..., 1:2, :], values[..., 0:1, :]], axis=-2)

    def zp_step(values):
        return f_swap(zp_flip(values), 2)

    steps = [zp_step]
    mask = n_et // 2
    while mask >= 1:
        steps.append(lambda values, mask=mask: e_swap(values, mask))
        mask //= 2

    def per_device(tokens, cotangent, route_experts, route_gates, w_gate, w_up, w_down):
        own_count, width = tokens.shape
        most = own_count // 8
        own_width, hidden_units = w_gate.shape
        half_units = hidden_units // 2
        f_index = lax.axis_index("fsdp")
        z_half = f_index // 4
        z_low = (f_index // 2) % 2
        y_index = f_index % 2

        chunks = chunk_list(half_units)
        keep_at = z_low * half_units
        give_at = (1 - z_low) * half_units

        def part_of(start, size):
            return jnp.stack(
                [
                    lax.dynamic_slice_in_dim(w_gate, start, size, axis=1),
                    lax.dynamic_slice_in_dim(w_up, start, size, axis=1),
                    lax.dynamic_slice_in_dim(w_down, start, size, axis=0).T,
                ]
            )

        count = len(chunks)
        kept, given = [], []
        for lo, size in chunks:
            kept.append(part_of(keep_at + lo, size))
            given.append(part_of(give_at + lo, size))
        near, far = [None] * count, [None] * count

        def start_pair(k):
            near[k] = jnp.concatenate([kept[k], f_swap(given[k], 2)], axis=1)

        first_far = f_swap(kept[0], 1)
        first_pair = f_swap(given[0], 2)
        near[0] = jnp.concatenate([kept[0], first_pair], axis=1)
        far[0] = jnp.concatenate([first_far, f_swap(first_pair, 1)], axis=1)
        for k in range(1, min(AHEAD, count)):
            start_pair(k)
            far[k] = f_swap(near[k], 1)

        own_start = lax.axis_index("et") * own_count
        own_experts = lax.dynamic_slice_in_dim(route_experts, own_start, own_count)
        own_gates = lax.dynamic_slice_in_dim(route_gates, own_start, own_count)
        is_first = own_experts[:, 0] == 0
        is_second = own_experts[:, 1] == 0
        chosen = jnp.logical_or(is_first, is_second)
        weight = jnp.where(is_first, own_gates[:, 0], 0.0) + jnp.where(
            is_second, own_gates[:, 1], 0.0
        )
        chosen_int = chosen.astype(jnp.int32)
        slot = jnp.cumsum(chosen_int) - chosen_int
        picks = jnp.logical_and(
            chosen[None, :], slot[None, :] == jnp.arange(most, dtype=jnp.int32)[:, None]
        )
        one_hot = picks.astype(BF16)
        packed_weight = jnp.sum(jnp.where(picks, weight[None, :], 0.0), axis=1)
        packed_rows = dot(one_hot, tokens).astype(BF16)
        packed_cot = (packed_weight[:, None] * dot(one_hot, cotangent)).astype(BF16)
        packed = jnp.concatenate([packed_rows, packed_cot], axis=0)

        cols = packed.reshape(2 * most, n_half, 2, 2, own_width)
        cols = jnp.where(z_low == 0, cols, cols[:, :, ::-1])
        cols = jnp.where(y_index == 0, cols, cols[:, :, :, ::-1])
        cols = jnp.transpose(cols, (1, 0, 3, 2, 4))
        blocks = []
        for d in range(n_half):
            block = lax.dynamic_index_in_dim(cols, z_half ^ d, 0, keepdims=False)
            blocks.append(block if d == 0 else f_swap(block, 4 * d))
        rows = jnp.stack(blocks)[None]
        for step in steps:
            rows = jnp.concatenate([rows, step(rows)], axis=0)
        members = rows.shape[0]
        slots = n_half * members * most
        rows = rows.reshape(members, n_half, 2, most, 2, 2 * own_width)
        rows = jnp.transpose(rows, (2, 4, 1, 0, 3, 5)).reshape(2, 2, slots, 2 * own_width)
        x_near, x_far, cot_near, cot_far = rows[0, 0], rows[0, 1], rows[1, 0], rows[1, 1]

        own_slots = slots // n_half
        total = None
        for k in range(count):
            units = kept[k].shape[2]
            near_k, far_k = near[k], far[k]
            gate = dot(x_near, near_k[0]) + dot(x_far, far_k[0])
            up = dot(x_near, near_k[1]) + dot(x_far, far_k[1])
            grad = dot(cot_near, near_k[2]) + dot(cot_far, far_k[2])
            part = jnp.concatenate([gate, up, grad], axis=1)
            sent = part[own_slots:].astype(BF16).reshape(n_half - 1, own_slots, 3 * units)
            if k + AHEAD < count:
                held = lax.optimization_barrier((kept[k + AHEAD], given[k + AHEAD], sent))
                kept[k + AHEAD], given[k + AHEAD], sent = held
                start_pair(k + AHEAD)
                far[k + AHEAD] = f_swap(near[k + AHEAD], 1)
            pre = part[:own_slots]
            for d in range(1, n_half):
                pre = pre + f_swap(sent[d - 1], 4 * d).astype(F32)
            gate, up, grad = pre[:, :units], pre[:, units : 2 * units], pre[:, 2 * units :]
            sig = jax.nn.sigmoid(gate)
            hidden = gate * sig * up
            grad_gate = grad * up * sig * (1.0 + gate * (1.0 - sig))
            grad_up = grad * gate * sig
            mine = jnp.concatenate([hidden, grad_gate, grad_up], axis=1).astype(BF16)
            full = jnp.concatenate([mine] + [f_swap(mine, 4 * d) for d in range(1, n_half)], axis=0)
            hidden, grad_gate, grad_up = (
                full[:, :units],
                full[:, units : 2 * units],
                full[:, 2 * units :],
            )
            terms = (
                dot_last(hidden, near_k[2]),
                dot_last(hidden, far_k[2]),
                dot_last(grad_gate, near_k[0]) + dot_last(grad_up, near_k[1]),
                dot_last(grad_gate, far_k[0]) + dot_last(grad_up, far_k[1]),
            )
            total = terms if total is None else tuple(a + b for a, b in zip(total, terms))

        sums = jnp.stack([jnp.stack(total[:2]), jnp.stack(total[2:])])
        sums = sums.reshape(2, 2, n_half, members, most, 2, own_width)
        sums = jnp.transpose(sums, (3, 2, 0, 4, 1, 5, 6))
        for step in reversed(steps):
            rest = sums.shape[0] // 2
            sums = sums[:rest] + step(sums[rest:].astype(BF16)).astype(F32)
        sums = sums[0].astype(BF16)
        back = [sums[0]] + [f_swap(sums[d], 4 * d) for d in range(1, n_half)]
        back = jnp.stack(back)
        order = jnp.arange(n_half, dtype=jnp.int32) ^ z_half
        back = jnp.take(back, order, axis=0)
        back = jnp.transpose(back, (1, 2, 0, 4, 3, 5))
        back = jnp.where(z_low == 0, back, back[:, :, :, ::-1])
        back = jnp.where(y_index == 0, back, back[:, :, :, :, ::-1])
        own_sums = back.reshape(2, most, width)
        spread = one_hot.T
        moe_out = (weight[:, None] * dot(spread, own_sums[0])).astype(BF16)
        grad_tokens = dot(spread, own_sums[1]).astype(BF16)
        return moe_out, grad_tokens

    return per_device


def call(body, outs, *args, scratch=(), flops=0):
    moved = sum(v.size * v.dtype.itemsize for v in list(args) + list(outs))
    return pl.pallas_call(
        body,
        out_shape=list(outs),
        scratch_shapes=list(scratch),
        compiler_params=pltpu.CompilerParams(vmem_limit_bytes=40 * 1024 * 1024),
        cost_estimate=pl.CostEstimate(flops=0, bytes_accessed=1024, transcendentals=0),
    )(*args)


def after(values, *others):
    return lax.optimization_barrier((values, *others))


def shaped(shape, kind):
    return jax.ShapeDtypeStruct(shape, kind)


def flip_pairs(values, own_width):
    parts = [values[..., i * own_width : (i + 1) * own_width] for i in (1, 0, 3, 2)]
    return jnp.concatenate(parts, axis=-1)


def route_columns(experts_ref, gates_ref):
    count = experts_ref.shape[0] // 4
    start = pl.multiple_of(lax.axis_index("et") * count, count)
    experts = experts_ref[pl.ds(start, count), :]
    gates = gates_ref[pl.ds(start, count), :]
    hits = (experts == 0).astype(F32)
    chosen = jnp.sum(hits, axis=1, keepdims=True)
    weight = jnp.sum(hits * gates, axis=1, keepdims=True)
    return chosen, weight


def as_row(column, keep):
    return jnp.sum(jnp.where(keep, column, 0.0), axis=0, keepdims=True)


def weight_chunk_body(low_ref, *refs):
    for gate, up, down, out in (refs[0:3] + refs[6:7], refs[3:6] + refs[7:8]):
        out[0] = gate[...]
        out[1] = up[...]
        out[2] = down[...].T


def weight_chunk(low, w_gate, w_up, w_down, lo, size):
    own_width, hidden_units = w_gate.shape
    half = hidden_units // 2 // size
    at = lo // size

    def spec(kept, rows):
        def index(i, low_ref):
            block = at + half * (low_ref[0] if kept else 1 - low_ref[0])
            return (block, 0) if rows else (0, block)

        return pl.BlockSpec((size, own_width) if rows else (own_width, size), index)

    out = shaped((3, own_width, size), BF16)
    specs = [spec(kept, rows) for kept in (True, False) for rows in (False, False, True)]
    whole = pl.BlockSpec((3, own_width, size), lambda i, low_ref: (0, 0, 0))
    return pl.pallas_call(
        weight_chunk_body,
        out_shape=[out, out],
        grid_spec=pltpu.PrefetchScalarGridSpec(
            num_scalar_prefetch=1, grid=(1,), in_specs=specs, out_specs=[whole, whole]
        ),
        compiler_params=pltpu.CompilerParams(vmem_limit_bytes=60 * 1024 * 1024),
        cost_estimate=pl.CostEstimate(
            flops=0, bytes_accessed=1024, transcendentals=0
        ),
    )(low, w_gate, w_up, w_down, w_gate, w_up, w_down)


def make_fused(n_fsdp, n_et):
    world = n_fsdp * n_et

    def swap(values, mask):
        pairs = [(i, i ^ mask) for i in range(world)]
        return lax.ppermute(values, ("fsdp", "et"), pairs)

    at_y, at_zp, at_zh = n_et, 2 * n_et, 4 * n_et
    at_core, at_x = 1, 2

    def per_device(tokens, cotangent, route_experts, route_gates, w_gate, w_up, w_down):
        own_count, width = tokens.shape
        most = own_count // 8
        own_width, hidden_units = w_gate.shape
        half_units = hidden_units // 2
        z_width = 4 * own_width
        block_shape = (2, most, z_width)
        low = ((lax.axis_index("fsdp") // 2) % 2).astype(jnp.int32).reshape(1)

        chunks = chunk_list(half_units)
        count = len(chunks)
        own_w, zp_w = [None] * count, [None] * count
        given = [None] * count

        stream = []

        def over_y(values):
            stream.append(swap(values, at_y))

        for k in range(count):
            own_w[k], given[k] = weight_chunk(
                low, w_gate, w_up, w_down, *chunks[k]
            )
        over_y(own_w[0])
        zp_w[0] = swap(given[0], at_zp)
        over_y(own_w[1])

        def pack_body(tokens_ref, cot_ref, experts_ref, gates_ref, keep_ref, send_ref, packed_ref):
            chosen, weight = route_columns(experts_ref, gates_ref)
            shape = (own_count, own_count)
            down = lax.broadcasted_iota(jnp.int32, shape, 0)
            across = lax.broadcasted_iota(jnp.int32, shape, 1)
            chosen_row = as_row(chosen, down == across)
            weight_row = as_row(weight, down == across)
            slot_row = as_row(chosen, down < across)
            places = lax.broadcasted_iota(jnp.int32, (most, own_count), 0).astype(F32)
            picks = jnp.logical_and(slot_row == places, chosen_row > 0.0)
            one_hot = jnp.where(picks, 1.0, 0.0).astype(BF16)
            slot_weight = jnp.sum(jnp.where(picks, weight_row, 0.0), axis=1, keepdims=True)
            packed_ref[0] = dot(one_hot, tokens_ref[...]).astype(BF16)
            packed_ref[1] = (slot_weight * dot(one_hot, cot_ref[...])).astype(BF16)
            f_index = lax.axis_index("fsdp")
            for d, out in enumerate((keep_ref, send_ref)):
                for i in range(4):
                    mask = 4 * d + 2 * (i % 2) + i // 2
                    start = pl.multiple_of((f_index ^ mask) * own_width, LANES)
                    columns = slice(i * own_width, (i + 1) * own_width)
                    out[:, :, columns] = packed_ref[:, :, pl.ds(start, own_width)]

        block = shaped(block_shape, BF16)
        mine, sent = call(
            pack_body,
            [block, block],
            tokens,
            cotangent,
            route_experts,
            route_gates,
            scratch=[pltpu.VMEM((2, most, width), BF16)],
            flops=4 * most * own_count * width,
        )
        other = swap(sent, at_zh)

        def join_body(mine_ref, other_ref, plain_ref, flipped_ref):
            for j, ref in enumerate((mine_ref, other_ref)):
                values = ref[...]
                plain_ref[j] = values
                flipped_ref[j] = flip_pairs(values, own_width)

        pair = shaped((2,) + block_shape, BF16)
        mine, zp_w[0], stream[0] = after(mine, zp_w[0], stream[0])
        plain, flipped = call(join_body, [pair, pair], mine, other)
        own_w[2], _ = after(own_w[2], plain)
        over_y(own_w[2])
        over_y(zp_w[0])
        for k in range(1, count):
            if k <= 2:
                given[k], _ = after(given[k], plain)
            else:
                given[k], zp_w[k - 2] = after(given[k], zp_w[k - 2])
            zp_w[k] = swap(given[k], at_zp)
        near_rows = jnp.stack(
            [plain, swap(plain, at_x), swap(flipped, at_zp), swap(flipped, at_zp + at_x)]
        )
        near_rows, stream[1] = after(near_rows, stream[1])
        far_rows = swap(near_rows, at_core)
        near_rows, stream[2], zp_w[1] = after(near_rows, stream[2], zp_w[1])
        over_y(zp_w[1])

        slots = 16 * most
        own_slots = slots // 2

        def rows_of(near_ref, far_ref, which):
            parts = [ref[:, :, which].reshape(own_slots, z_width) for ref in (near_ref, far_ref)]
            return jnp.concatenate(parts, axis=0)

        def first_body(near_ref, far_ref, a_ref, b_ref, c_ref, d_ref, keep_ref, send_ref):
            units = a_ref.shape[2]
            rows = rows_of(near_ref, far_ref, 0)
            cots = rows_of(near_ref, far_ref, 1)
            for j in range(3):
                left = cots if j == 2 else rows
                value = None
                for i, ref in enumerate((a_ref, b_ref, c_ref, d_ref)):
                    term = dot(left[:, i * own_width : (i + 1) * own_width], ref[j])
                    value = term if value is None else value + term
                value = value.reshape(8, 2, most, units)
                columns = slice(j * units, (j + 1) * units)
                keep_ref[:, columns] = value[:, 0].reshape(own_slots, units)
                send_ref[:, columns] = value[:, 1].reshape(own_slots, units).astype(BF16)

        def middle_body(keep_ref, recv_ref, out_ref):
            units = keep_ref.shape[1] // 3
            pre = keep_ref[...] + recv_ref[...].astype(F32)
            gate, up, grad = pre[:, :units], pre[:, units : 2 * units], pre[:, 2 * units :]
            sig = 1.0 / (1.0 + jnp.exp(-gate))
            out_ref[:, :units] = (gate * sig * up).astype(BF16)
            out_ref[:, units : 2 * units] = (
                grad * up * sig * (1.0 + gate * (1.0 - sig))
            ).astype(BF16)
            out_ref[:, 2 * units :] = (grad * gate * sig).astype(BF16)

        def second_terms(mine_ref, recv_ref, refs):
            units = refs[0].shape[2]
            full = jnp.concatenate([mine_ref[...], recv_ref[...]], axis=0)
            hidden, grad_gate, grad_up = (
                full[:, j * units : (j + 1) * units] for j in range(3)
            )
            outs = [dot_last(hidden, ref[2]) for ref in refs]
            grads = [dot_last(grad_gate, ref[0]) + dot_last(grad_up, ref[1]) for ref in refs]
            return outs, grads

        def second_body(first, last, mine_ref, recv_ref, a_ref, b_ref, c_ref, d_ref, *rest):
            terms = second_terms(mine_ref, recv_ref, (a_ref, b_ref, c_ref, d_ref))
            rest = list(rest)
            held = None if first else rest.pop(0)
            for which in range(2):
                for i in range(4):
                    columns = slice(i * own_width, (i + 1) * own_width)
                    value = terms[which][i]
                    if held is not None:
                        value = value + held[which, :, columns]
                    if not last:
                        rest[0][which, :, columns] = value
                        continue
                    value = value.reshape(2, 2, 4, most, own_width)
                    for j in range(2):
                        rest[0][:, j, which, :, columns] = value[j, 0]
                        rest[1][:, j, which, :, columns] = value[j, 1].astype(BF16)

        quad = (4, 2) + block_shape
        pre, mine, total = [None] * count, [None] * count, [None] * count

        def weights_of(k):
            at = (k, k + 3) if k < 3 else (2 * k, 2 * k + 1)
            return own_w[k], zp_w[k], stream[at[0]], stream[at[1]]

        def first(k, near_rows, far_rows):
            units = chunks[k][1]
            pre[k] = call(
                first_body,
                [shaped((own_slots, 3 * units), F32), shaped((own_slots, 3 * units), BF16)],
                near_rows,
                far_rows,
                *weights_of(k),
            )

        def middle(k):
            units = chunks[k][1]
            keep, sent = pre[k]
            (mine[k],) = call(
                middle_body,
                [shaped((own_slots, 3 * units), BF16)],
                keep,
                swap(sent, at_zh),
            )

        def second(k):
            is_first, is_last = k == 0, k == count - 1
            outs = (
                [shaped(quad, F32), shaped(quad, BF16)]
                if is_last
                else [shaped((2, slots, z_width), F32)]
            )
            held = () if is_first else total[k - 1]
            total[k] = call(
                lambda *refs: second_body(is_first, is_last, *refs),
                outs,
                mine[k],
                swap(mine[k], at_zh),
                *weights_of(k),
                *held,
            )

        def held_back(values, firsts=(), middles=(), seconds=()):
            middles = [k for k in middles if k >= 0]
            seconds = [k for k in seconds if k >= 0]
            done = [pre[k][1] for k in firsts] + [mine[k] for k in middles]
            done += [total[k][0] for k in seconds]
            values, *done = after(values, *done)
            for k in firsts:
                pre[k] = [pre[k][0], done.pop(0)]
            for k in middles:
                mine[k] = done.pop(0)
            for k in seconds:
                total[k] = [done.pop(0)]
            return values

        def own_over_y(k, *steps):
            own_w[k] = held_back(own_w[k], *steps)
            over_y(own_w[k])

        def pair_over_y(k, *steps):
            zp_w[k] = held_back(zp_w[k], *steps)
            over_y(zp_w[k])

        first(0, near_rows, far_rows)
        pair_over_y(2, [0])
        first(1, near_rows, far_rows)
        own_over_y(3, [1])
        pair_over_y(3, [1])
        middle(0)
        second(0)
        first(2, held_back(near_rows, [], [0]), far_rows)
        own_over_y(4, [2])
        pair_over_y(4, [2])
        middle(1)
        second(1)
        pre[2] = [held_back(pre[2][0], [], [1], [0]), pre[2][1]]
        middle(2)
        second(2)
        first(3, held_back(near_rows, [], [2], [1]), far_rows)
        first(4, held_back(near_rows, [3], [], [2]), far_rows)
        pre[3] = [held_back(pre[3][0], [4]), pre[3][1]]
        middle(3)
        second(3)
        middle(4)
        second(4)
        total = total[-1]

        def spread_body(keep_ref, recv_ref, own_ref, *outs):
            value = keep_ref[...] + recv_ref[...].astype(F32)
            own_ref[...] = value[0]
            for i in range(1, 4):
                part = value[i].astype(BF16)
                outs[i - 1][...] = flip_pairs(part, own_width) if i >= 2 else part

        keep, sent = total
        own, by_x, by_zp, by_both = call(
            spread_body,
            [shaped(pair.shape, F32), pair, pair, pair],
            keep,
            swap(sent, at_core),
        )

        def gather_body(own_ref, x_ref, zp_ref, both_ref, keep_ref, send_ref):
            value = own_ref[...] + x_ref[...].astype(F32)
            value = value + (zp_ref[...].astype(F32) + both_ref[...].astype(F32))
            keep_ref[...] = value[0].astype(BF16)
            send_ref[...] = value[1].astype(BF16)

        mine, sent = call(
            gather_body,
            [block, block],
            own,
            swap(by_x, at_x),
            swap(by_zp, at_zp),
            swap(by_both, at_zp + at_x),
        )

        def unpack_body(mine_ref, other_ref, experts_ref, gates_ref, out_ref, grad_ref, sums_ref):
            f_index = lax.axis_index("fsdp")
            for d, ref in enumerate((mine_ref, other_ref)):
                for i in range(4):
                    mask = 4 * d + 2 * (i % 2) + i // 2
                    start = pl.multiple_of((f_index ^ mask) * own_width, LANES)
                    columns = slice(i * own_width, (i + 1) * own_width)
                    sums_ref[:, :, pl.ds(start, own_width)] = ref[:, :, columns]
            chosen, weight = route_columns(experts_ref, gates_ref)
            shape = (own_count, own_count)
            down = lax.broadcasted_iota(jnp.int32, shape, 0)
            across = lax.broadcasted_iota(jnp.int32, shape, 1)
            chosen_row = as_row(chosen, down == across)
            slot = jnp.sum(jnp.where(across < down, chosen_row, 0.0), axis=1, keepdims=True)
            places = lax.broadcasted_iota(jnp.int32, (own_count, most), 1).astype(F32)
            picks = jnp.logical_and(slot == places, chosen > 0.0)
            spread = jnp.where(picks, 1.0, 0.0).astype(BF16)
            out_ref[...] = (weight * dot(spread, sums_ref[0])).astype(BF16)
            grad_ref[...] = dot(spread, sums_ref[1]).astype(BF16)

        result = shaped(tokens.shape, BF16)
        return tuple(
            call(
                unpack_body,
                [result, result],
                mine,
                swap(sent, at_zh),
                route_experts,
                route_gates,
                scratch=[pltpu.VMEM((2, most, width), BF16)],
                flops=4 * most * own_count * width,
            )
        )

    return per_device


def solution(mesh):
    sizes = dict(mesh.shape)
    make = make_fused if sizes["fsdp"] == 8 and sizes["et"] == 4 else make_plain
    in_specs = (
        P(("fsdp", "et"), None),
        P(("fsdp", "et"), None),
        P("fsdp", None),
        P("fsdp", None),
        P("fsdp", "et"),
        P("fsdp", "et"),
        P("et", "fsdp"),
    )
    out_specs = (P(("fsdp", "et"), None), P(("fsdp", "et"), None))
    return jax.shard_map(
        make(sizes["fsdp"], sizes["et"]),
        mesh=mesh,
        in_specs=in_specs,
        out_specs=out_specs,
        check_vma=False,
    )
```

```python
import jax
import jax.numpy as jnp
from jax import lax
from jax.experimental import pallas as pl
from jax.experimental.pallas import tpu as pltpu
from jax.sharding import PartitionSpec as P

F32 = jnp.float32
SHAPE = ((0, 1), (2, 2), (4, 2), (6, 2), (1, 1))
CFG = {'us': [8, 0], 'flags': {'join_y0': True, 'join_zp0': True, 'own2_plain': True, 'near_y1': True, 'near_y2': False, 'near_y3': False, 'near_zp1': False, 'first_y2': True, 'first_zp1': True}, 'order': [('F', 0), ('F', 1), ('S', 0), ('F', 2), ('S', 1), ('F', 3), ('S', 2), ('F', 4), ('S', 3), ('S', 4)], 'ties': {('F', 1): [('F', 0)], ('F', 2): [('F', 1)], ('S', 0): [('F', 1)], ('F', 3): [('S', 0)], ('S', 1): [('F', 2)], ('F', 4): [('S', 1), ('F', 3)], ('S', 2): [('F', 3)], ('S', 3): [('F', 4)]}, 'y': {5: [('F', 0)], 6: [('F', 1)], 7: [('F', 1)], 8: [('F', 2)], 9: [('F', 2)]}, 'arrive': {}}
BF16 = jnp.bfloat16
LANES = 128
AHEAD = 2


def dot(left, right):
    return jnp.dot(left, right, preferred_element_type=F32)


def dot_last(left, right):
    return lax.dot_general(left, right, (((1,), (1,)), ((), ())), preferred_element_type=F32)


def chunk_list(units):
    blocks = units // LANES
    if blocks != 8:
        return [(i * LANES, LANES) for i in range(blocks)]
    shape = SHAPE
    return [(start * LANES, size * LANES) for start, size in shape]


def make_plain(n_fsdp, n_et):
    n_half = n_fsdp // 4

    def f_swap(values, mask):
        return lax.ppermute(values, "fsdp", [(f, f ^ mask) for f in range(n_fsdp)])

    def e_swap(values, mask):
        return lax.ppermute(values, "et", [(e, e ^ mask) for e in range(n_et)])

    def zp_flip(values):
        return jnp.concatenate([values[..., 1:2, :], values[..., 0:1, :]], axis=-2)

    def zp_step(values):
        return f_swap(zp_flip(values), 2)

    steps = [zp_step]
    mask = n_et // 2
    while mask >= 1:
        steps.append(lambda values, mask=mask: e_swap(values, mask))
        mask //= 2

    def per_device(tokens, cotangent, route_experts, route_gates, w_gate, w_up, w_down):
        own_count, width = tokens.shape
        most = own_count // 8
        own_width, hidden_units = w_gate.shape
        half_units = hidden_units // 2
        f_index = lax.axis_index("fsdp")
        z_half = f_index // 4
        z_low = (f_index // 2) % 2
        y_index = f_index % 2

        chunks = chunk_list(half_units)
        keep_at = z_low * half_units
        give_at = (1 - z_low) * half_units

        def part_of(start, size):
            return jnp.stack(
                [
                    lax.dynamic_slice_in_dim(w_gate, start, size, axis=1),
                    lax.dynamic_slice_in_dim(w_up, start, size, axis=1),
                    lax.dynamic_slice_in_dim(w_down, start, size, axis=0).T,
                ]
            )

        count = len(chunks)
        kept, given = [], []
        for lo, size in chunks:
            kept.append(part_of(keep_at + lo, size))
            given.append(part_of(give_at + lo, size))
        near, far = [None] * count, [None] * count

        def start_pair(k):
            near[k] = jnp.concatenate([kept[k], f_swap(given[k], 2)], axis=1)

        first_far = f_swap(kept[0], 1)
        first_pair = f_swap(given[0], 2)
        near[0] = jnp.concatenate([kept[0], first_pair], axis=1)
        far[0] = jnp.concatenate([first_far, f_swap(first_pair, 1)], axis=1)
        for k in range(1, min(AHEAD, count)):
            start_pair(k)
            far[k] = f_swap(near[k], 1)

        own_start = lax.axis_index("et") * own_count
        own_experts = lax.dynamic_slice_in_dim(route_experts, own_start, own_count)
        own_gates = lax.dynamic_slice_in_dim(route_gates, own_start, own_count)
        is_first = own_experts[:, 0] == 0
        is_second = own_experts[:, 1] == 0
        chosen = jnp.logical_or(is_first, is_second)
        weight = jnp.where(is_first, own_gates[:, 0], 0.0) + jnp.where(
            is_second, own_gates[:, 1], 0.0
        )
        chosen_int = chosen.astype(jnp.int32)
        slot = jnp.cumsum(chosen_int) - chosen_int
        picks = jnp.logical_and(
            chosen[None, :], slot[None, :] == jnp.arange(most, dtype=jnp.int32)[:, None]
        )
        one_hot = picks.astype(BF16)
        packed_weight = jnp.sum(jnp.where(picks, weight[None, :], 0.0), axis=1)
        packed_rows = dot(one_hot, tokens).astype(BF16)
        packed_cot = (packed_weight[:, None] * dot(one_hot, cotangent)).astype(BF16)
        packed = jnp.concatenate([packed_rows, packed_cot], axis=0)

        cols = packed.reshape(2 * most, n_half, 2, 2, own_width)
        cols = jnp.where(z_low == 0, cols, cols[:, :, ::-1])
        cols = jnp.where(y_index == 0, cols, cols[:, :, :, ::-1])
        cols = jnp.transpose(cols, (1, 0, 3, 2, 4))
        blocks = []
        for d in range(n_half):
            block = lax.dynamic_index_in_dim(cols, z_half ^ d, 0, keepdims=False)
            blocks.append(block if d == 0 else f_swap(block, 4 * d))
        rows = jnp.stack(blocks)[None]
        for step in steps:
            rows = jnp.concatenate([rows, step(rows)], axis=0)
        members = rows.shape[0]
        slots = n_half * members * most
        rows = rows.reshape(members, n_half, 2, most, 2, 2 * own_width)
        rows = jnp.transpose(rows, (2, 4, 1, 0, 3, 5)).reshape(2, 2, slots, 2 * own_width)
        x_near, x_far, cot_near, cot_far = rows[0, 0], rows[0, 1], rows[1, 0], rows[1, 1]

        own_slots = slots // n_half
        total = None
        for k in range(count):
            units = kept[k].shape[2]
            near_k, far_k = near[k], far[k]
            gate = dot(x_near, near_k[0]) + dot(x_far, far_k[0])
            up = dot(x_near, near_k[1]) + dot(x_far, far_k[1])
            grad = dot(cot_near, near_k[2]) + dot(cot_far, far_k[2])
            part = jnp.concatenate([gate, up, grad], axis=1)
            sent = part[own_slots:].astype(BF16).reshape(n_half - 1, own_slots, 3 * units)
            if k + AHEAD < count:
                held = lax.optimization_barrier((kept[k + AHEAD], given[k + AHEAD], sent))
                kept[k + AHEAD], given[k + AHEAD], sent = held
                start_pair(k + AHEAD)
                far[k + AHEAD] = f_swap(near[k + AHEAD], 1)
            pre = part[:own_slots]
            for d in range(1, n_half):
                pre = pre + f_swap(sent[d - 1], 4 * d).astype(F32)
            gate, up, grad = pre[:, :units], pre[:, units : 2 * units], pre[:, 2 * units :]
            sig = jax.nn.sigmoid(gate)
            hidden = gate * sig * up
            grad_gate = grad * up * sig * (1.0 + gate * (1.0 - sig))
            grad_up = grad * gate * sig
            mine = jnp.concatenate([hidden, grad_gate, grad_up], axis=1).astype(BF16)
            full = jnp.concatenate([mine] + [f_swap(mine, 4 * d) for d in range(1, n_half)], axis=0)
            hidden, grad_gate, grad_up = (
                full[:, :units],
                full[:, units : 2 * units],
                full[:, 2 * units :],
            )
            terms = (
                dot_last(hidden, near_k[2]),
                dot_last(hidden, far_k[2]),
                dot_last(grad_gate, near_k[0]) + dot_last(grad_up, near_k[1]),
                dot_last(grad_gate, far_k[0]) + dot_last(grad_up, far_k[1]),
            )
            total = terms if total is None else tuple(a + b for a, b in zip(total, terms))

        sums = jnp.stack([jnp.stack(total[:2]), jnp.stack(total[2:])])
        sums = sums.reshape(2, 2, n_half, members, most, 2, own_width)
        sums = jnp.transpose(sums, (3, 2, 0, 4, 1, 5, 6))
        for step in reversed(steps):
            rest = sums.shape[0] // 2
            sums = sums[:rest] + step(sums[rest:].astype(BF16)).astype(F32)
        sums = sums[0].astype(BF16)
        back = [sums[0]] + [f_swap(sums[d], 4 * d) for d in range(1, n_half)]
        back = jnp.stack(back)
        order = jnp.arange(n_half, dtype=jnp.int32) ^ z_half
        back = jnp.take(back, order, axis=0)
        back = jnp.transpose(back, (1, 2, 0, 4, 3, 5))
        back = jnp.where(z_low == 0, back, back[:, :, :, ::-1])
        back = jnp.where(y_index == 0, back, back[:, :, :, :, ::-1])
        own_sums = back.reshape(2, most, width)
        spread = one_hot.T
        moe_out = (weight[:, None] * dot(spread, own_sums[0])).astype(BF16)
        grad_tokens = dot(spread, own_sums[1]).astype(BF16)
        return moe_out, grad_tokens

    return per_device


def call(body, outs, *args, scratch=(), flops=0, us=0):
    moved = sum(v.size * v.dtype.itemsize for v in list(args) + list(outs))
    return pl.pallas_call(
        body,
        out_shape=list(outs),
        scratch_shapes=list(scratch),
        compiler_params=pltpu.CompilerParams(vmem_limit_bytes=40 * 1024 * 1024),
        cost_estimate=pl.CostEstimate(flops=us * 1000000000, bytes_accessed=1024, transcendentals=0),
    )(*args)


def after(values, *others):
    return lax.optimization_barrier((values, *others))


def shaped(shape, kind):
    return jax.ShapeDtypeStruct(shape, kind)


def flip_pairs(values, own_width):
    parts = [values[..., i * own_width : (i + 1) * own_width] for i in (1, 0, 3, 2)]
    return jnp.concatenate(parts, axis=-1)


def route_columns(experts_ref, gates_ref):
    count = experts_ref.shape[0] // 4
    start = pl.multiple_of(lax.axis_index("et") * count, count)
    experts = experts_ref[pl.ds(start, count), :]
    gates = gates_ref[pl.ds(start, count), :]
    hits = (experts == 0).astype(F32)
    chosen = jnp.sum(hits, axis=1, keepdims=True)
    weight = jnp.sum(hits * gates, axis=1, keepdims=True)
    return chosen, weight


def as_row(column, keep):
    return jnp.sum(jnp.where(keep, column, 0.0), axis=0, keepdims=True)


def weight_chunk_body(low_ref, *refs):
    for gate, up, down, out in (refs[0:3] + refs[6:7], refs[3:6] + refs[7:8]):
        out[0] = gate[...]
        out[1] = up[...]
        out[2] = down[...].T


def weight_chunk(low, w_gate, w_up, w_down, lo, size):
    own_width, hidden_units = w_gate.shape
    half = hidden_units // 2 // size
    at = lo // size

    def spec(kept, rows):
        def index(i, low_ref):
            block = at + half * (low_ref[0] if kept else 1 - low_ref[0])
            return (block, 0) if rows else (0, block)

        return pl.BlockSpec((size, own_width) if rows else (own_width, size), index)

    out = shaped((3, own_width, size), BF16)
    specs = [spec(kept, rows) for kept in (True, False) for rows in (False, False, True)]
    whole = pl.BlockSpec((3, own_width, size), lambda i, low_ref: (0, 0, 0))
    return pl.pallas_call(
        weight_chunk_body,
        out_shape=[out, out],
        grid_spec=pltpu.PrefetchScalarGridSpec(
            num_scalar_prefetch=1, grid=(1,), in_specs=specs, out_specs=[whole, whole]
        ),
        compiler_params=pltpu.CompilerParams(vmem_limit_bytes=60 * 1024 * 1024),
        cost_estimate=pl.CostEstimate(
            flops=0, bytes_accessed=1024, transcendentals=0
        ),
    )(low, w_gate, w_up, w_down, w_gate, w_up, w_down)


def make_fused(n_fsdp, n_et):
    world = n_fsdp * n_et

    def swap(values, mask):
        pairs = [(i, i ^ mask) for i in range(world)]
        return lax.ppermute(values, ("fsdp", "et"), pairs)

    at_y, at_zp, at_zh = n_et, 2 * n_et, 4 * n_et
    at_core, at_x = 1, 2

    def per_device(tokens, cotangent, route_experts, route_gates, w_gate, w_up, w_down):
        own_count, width = tokens.shape
        most = own_count // 8
        own_width, hidden_units = w_gate.shape
        half_units = hidden_units // 2
        z_width = 4 * own_width
        block_shape = (2, most, z_width)
        low = ((lax.axis_index("fsdp") // 2) % 2).astype(jnp.int32).reshape(1)

        chunks = chunk_list(half_units)
        count = len(chunks)
        own_w, zp_w = [None] * count, [None] * count
        given = [None] * count

        stream = []

        def over_y(values):
            stream.append(swap(values, at_y))

        for k in range(count):
            own_w[k], given[k] = weight_chunk(
                low, w_gate, w_up, w_down, *chunks[k]
            )
        over_y(own_w[0])
        zp_w[0] = swap(given[0], at_zp)
        over_y(own_w[1])

        def pack_body(tokens_ref, cot_ref, experts_ref, gates_ref, keep_ref, send_ref, packed_ref):
            chosen, weight = route_columns(experts_ref, gates_ref)
            shape = (own_count, own_count)
            down = lax.broadcasted_iota(jnp.int32, shape, 0)
            across = lax.broadcasted_iota(jnp.int32, shape, 1)
            chosen_row = as_row(chosen, down == across)
            weight_row = as_row(weight, down == across)
            slot_row = as_row(chosen, down < across)
            places = lax.broadcasted_iota(jnp.int32, (most, own_count), 0).astype(F32)
            picks = jnp.logical_and(slot_row == places, chosen_row > 0.0)
            one_hot = jnp.where(picks, 1.0, 0.0).astype(BF16)
            slot_weight = jnp.sum(jnp.where(picks, weight_row, 0.0), axis=1, keepdims=True)
            packed_ref[0] = dot(one_hot, tokens_ref[...]).astype(BF16)
            packed_ref[1] = (slot_weight * dot(one_hot, cot_ref[...])).astype(BF16)
            f_index = lax.axis_index("fsdp")
            for d, out in enumerate((keep_ref, send_ref)):
                for i in range(4):
                    mask = 4 * d + 2 * (i % 2) + i // 2
                    start = pl.multiple_of((f_index ^ mask) * own_width, LANES)
                    columns = slice(i * own_width, (i + 1) * own_width)
                    out[:, :, columns] = packed_ref[:, :, pl.ds(start, own_width)]

        block = shaped(block_shape, BF16)
        mine, sent = call(
            pack_body,
            [block, block],
            tokens,
            cotangent,
            route_experts,
            route_gates,
            scratch=[pltpu.VMEM((2, most, width), BF16)],
            flops=4 * most * own_count * width,
        )
        other = swap(sent, at_zh)

        def join_body(mine_ref, other_ref, plain_ref, flipped_ref):
            for j, ref in enumerate((mine_ref, other_ref)):
                values = ref[...]
                plain_ref[j] = values
                flipped_ref[j] = flip_pairs(values, own_width)

        pair = shaped((2,) + block_shape, BF16)
        if CFG["flags"]["join_y0"]:
            mine, stream[0] = after(mine, stream[0])
        if CFG["flags"]["join_zp0"]:
            mine, zp_w[0] = after(mine, zp_w[0])
        plain, flipped = call(join_body, [pair, pair], mine, other)
        if CFG["flags"]["own2_plain"]:
            own_w[2], _ = after(own_w[2], plain)
        over_y(own_w[2])
        over_y(zp_w[0])
        for k in range(1, count):
            if k <= 2:
                given[k], _ = after(given[k], plain)
            else:
                given[k], zp_w[k - 2] = after(given[k], zp_w[k - 2])
            zp_w[k] = swap(given[k], at_zp)
        near_rows = jnp.stack(
            [plain, swap(plain, at_x), swap(flipped, at_zp), swap(flipped, at_zp + at_x)]
        )
        for at in (1, 2, 3):
            if CFG["flags"][f"near_y{at}"]:
                near_rows, stream[at] = after(near_rows, stream[at])
        if CFG["flags"]["near_zp1"]:
            near_rows, zp_w[1] = after(near_rows, zp_w[1])
        far_rows = swap(near_rows, at_core)
        for at in (2,):
            if CFG["flags"]["first_y2"]:
                near_rows, stream[at] = after(near_rows, stream[at])
        if CFG["flags"]["first_zp1"]:
            near_rows, zp_w[1] = after(near_rows, zp_w[1])
        over_y(zp_w[1])

        slots = 16 * most
        own_slots = slots // 2

        def rows_of(near_ref, far_ref, which):
            parts = [ref[:, :, which].reshape(own_slots, z_width) for ref in (near_ref, far_ref)]
            return jnp.concatenate(parts, axis=0)

        def first_body(near_ref, far_ref, a_ref, b_ref, c_ref, d_ref, keep_ref, send_ref):
            units = a_ref.shape[2]
            rows = rows_of(near_ref, far_ref, 0)
            cots = rows_of(near_ref, far_ref, 1)
            for j in range(3):
                left = cots if j == 2 else rows
                value = None
                for i, ref in enumerate((a_ref, b_ref, c_ref, d_ref)):
                    term = dot(left[:, i * own_width : (i + 1) * own_width], ref[j])
                    value = term if value is None else value + term
                columns = slice(j * units, (j + 1) * units)
                keep_ref[:, columns] = value
                value = value.astype(BF16).reshape(8, 2, most, units)
                value = jnp.concatenate([value[:, 1:2], value[:, 0:1]], axis=1)
                send_ref[:, columns] = value.reshape(slots, units)

        def second_terms(keep_ref, recv_ref, refs):
            units = refs[0].shape[2]
            pre = keep_ref[...] + recv_ref[...].astype(F32)
            gate, up, grad = pre[:, :units], pre[:, units : 2 * units], pre[:, 2 * units :]
            sig = 1.0 / (1.0 + jnp.exp(-gate))
            hidden = (gate * sig * up).astype(BF16)
            grad_gate = (grad * up * sig * (1.0 + gate * (1.0 - sig))).astype(BF16)
            grad_up = (grad * gate * sig).astype(BF16)
            outs = [dot_last(hidden, ref[2]) for ref in refs]
            grads = [dot_last(grad_gate, ref[0]) + dot_last(grad_up, ref[1]) for ref in refs]
            return outs, grads

        def second_body(first, last, keep_ref, recv_ref, a_ref, b_ref, c_ref, d_ref, *rest):
            terms = second_terms(keep_ref, recv_ref, (a_ref, b_ref, c_ref, d_ref))
            rest = list(rest)
            held = None if first else rest.pop(0)
            for which in range(2):
                for i in range(4):
                    columns = slice(i * own_width, (i + 1) * own_width)
                    value = terms[which][i]
                    if held is not None:
                        value = value + held[which, :, columns]
                    if not last:
                        rest[0][which, :, columns] = value
                        continue
                    value = value.reshape(2, 4, 2, most, own_width)
                    for j in range(2):
                        rest[0][:, j, which, :, columns] = value[0, :, j]
                        rest[1][:, j, which, :, columns] = value[1, :, j].astype(BF16)

        quad = (4, 2) + block_shape
        pre, total = [None] * count, [None] * count

        def weights_of(k):
            at = (k, k + 3) if k < 3 else (2 * k, 2 * k + 1)
            return own_w[k], zp_w[k], stream[at[0]], stream[at[1]]

        def first(k, near_rows, far_rows):
            units = chunks[k][1]
            pre[k] = call(
                first_body,
                [shaped((slots, 3 * units), F32), shaped((slots, 3 * units), BF16)],
                near_rows,
                far_rows,
                *weights_of(k),
                us=CFG["us"][0] * units // 256,
            )

        def second(k):
            is_first, is_last = k == 0, k == count - 1
            outs = (
                [shaped(quad, F32), shaped(quad, BF16)]
                if is_last
                else [shaped((2, slots, z_width), F32)]
            )
            held = () if is_first else total[k - 1]
            keep, sent = pre[k]
            total[k] = call(
                lambda *refs: second_body(is_first, is_last, *refs),
                outs,
                keep,
                swap(sent, at_zh),
                *weights_of(k),
                *held,
                us=CFG["us"][1],
            )

        def held_back(values, firsts=(), seconds=()):
            done = [pre[k][1] for k in firsts] + [total[k][0] for k in seconds]
            if not done:
                return values
            values, *done = after(values, *done)
            for k in firsts:
                pre[k] = [pre[k][0], done.pop(0)]
            for k in seconds:
                total[k] = [done.pop(0)]
            return values

        def steps_of(names):
            return [[k for kind, k in names if kind == want] for want in "FS"]

        def emit_y(j):
            k = j // 2
            values = zp_w if (j % 2 or k < 3) else own_w
            k = j - 3 if j < 6 else k
            values[k] = held_back(values[k], *steps_of(CFG["y"][j]))
            over_y(values[k])

        pending = [5, 6, 7, 8, 9]
        done_ops = []
        while pending and not CFG["y"][pending[0]]:
            emit_y(pending.pop(0))
        for kind, k in CFG["order"]:
            ties = steps_of(CFG["ties"].get((kind, k), []))
            late = CFG["arrive"].get((kind, k), [])
            values = near_rows if kind == "F" else pre[k][0]
            if any(ties):
                values = held_back(values, *ties)
            for at in late:
                values, stream[at] = after(values, stream[at])
            if kind == "F":
                first(k, values, far_rows)
            else:
                pre[k] = [values, pre[k][1]]
                second(k)
            done_ops.append((kind, k))
            while pending and all(op in done_ops for op in CFG["y"][pending[0]]):
                emit_y(pending.pop(0))
        total = total[-1]

        def spread_body(keep_ref, recv_ref, own_ref, *outs):
            value = keep_ref[...] + recv_ref[...].astype(F32)
            own_ref[...] = value[0]
            for i in range(1, 4):
                part = value[i].astype(BF16)
                outs[i - 1][...] = flip_pairs(part, own_width) if i >= 2 else part

        keep, sent = total
        own, by_x, by_zp, by_both = call(
            spread_body,
            [shaped(pair.shape, F32), pair, pair, pair],
            keep,
            swap(sent, at_core),
        )

        def gather_body(own_ref, x_ref, zp_ref, both_ref, keep_ref, send_ref):
            value = own_ref[...] + x_ref[...].astype(F32)
            value = value + (zp_ref[...].astype(F32) + both_ref[...].astype(F32))
            keep_ref[...] = value[0].astype(BF16)
            send_ref[...] = value[1].astype(BF16)

        mine, sent = call(
            gather_body,
            [block, block],
            own,
            swap(by_x, at_x),
            swap(by_zp, at_zp),
            swap(by_both, at_zp + at_x),
        )

        def unpack_body(mine_ref, other_ref, experts_ref, gates_ref, out_ref, grad_ref, sums_ref):
            f_index = lax.axis_index("fsdp")
            for d, ref in enumerate((mine_ref, other_ref)):
                for i in range(4):
                    mask = 4 * d + 2 * (i % 2) + i // 2
                    start = pl.multiple_of((f_index ^ mask) * own_width, LANES)
                    columns = slice(i * own_width, (i + 1) * own_width)
                    sums_ref[:, :, pl.ds(start, own_width)] = ref[:, :, columns]
            chosen, weight = route_columns(experts_ref, gates_ref)
            shape = (own_count, own_count)
            down = lax.broadcasted_iota(jnp.int32, shape, 0)
            across = lax.broadcasted_iota(jnp.int32, shape, 1)
            chosen_row = as_row(chosen, down == across)
            slot = jnp.sum(jnp.where(across < down, chosen_row, 0.0), axis=1, keepdims=True)
            places = lax.broadcasted_iota(jnp.int32, (own_count, most), 1).astype(F32)
            picks = jnp.logical_and(slot == places, chosen > 0.0)
            spread = jnp.where(picks, 1.0, 0.0).astype(BF16)
            out_ref[...] = (weight * dot(spread, sums_ref[0])).astype(BF16)
            grad_ref[...] = dot(spread, sums_ref[1]).astype(BF16)

        result = shaped(tokens.shape, BF16)
        return tuple(
            call(
                unpack_body,
                [result, result],
                mine,
                swap(sent, at_zh),
                route_experts,
                route_gates,
                scratch=[pltpu.VMEM((2, most, width), BF16)],
                flops=4 * most * own_count * width,
            )
        )

    return per_device


def solution(mesh):
    sizes = dict(mesh.shape)
    make = make_fused if sizes["fsdp"] == 8 and sizes["et"] == 4 else make_plain
    in_specs = (
        P(("fsdp", "et"), None),
        P(("fsdp", "et"), None),
        P("fsdp", None),
        P("fsdp", None),
        P("fsdp", "et"),
        P("fsdp", "et"),
        P("et", "fsdp"),
    )
    out_specs = (P(("fsdp", "et"), None), P(("fsdp", "et"), None))
    return jax.shard_map(
        make(sizes["fsdp"], sizes["et"]),
        mesh=mesh,
        in_specs=in_specs,
        out_specs=out_specs,
        check_vma=False,
    )
```

```python
import jax
import jax.numpy as jnp
from jax import lax
from jax.experimental import pallas as pl
from jax.experimental.pallas import tpu as pltpu
from jax.sharding import PartitionSpec as P

F32 = jnp.float32
SHAPE = ((0, 1), (2, 2), (4, 2), (1, 1), (6, 1), (7, 1))
CFG = {'us': [8, 0], 'flags': {'join_y0': True, 'join_zp0': True, 'own2_plain': True, 'near_y1': True, 'near_y2': False, 'near_y3': False, 'near_zp1': False, 'first_y2': True, 'first_zp1': True, 'zp0_early': True}, 'order': [('F', 0), ('F', 1), ('S', 0), ('F', 2), ('S', 1), ('F', 3), ('S', 2), ('F', 4), ('S', 3), ('F', 5), ('S', 4), ('S', 5)], 'ties': {('F', 1): [('F', 0)], ('F', 2): [('F', 1)], ('S', 0): [('F', 1)], ('F', 3): [('S', 0)], ('S', 1): [('F', 2)], ('F', 4): [('S', 1), ('F', 3)], ('F', 5): [('S', 3), ('F', 4)], ('S', 3): [('F', 4)], ('S', 4): [('F', 5)]}, 'y': {5: [('F', 0)], 6: [('F', 1)], 7: [('F', 1)], 8: [('F', 2)], 9: [('F', 2)], 10: [('F', 3)], 11: [('F', 3)]}, 'zp': {3: [('F', 0)], 4: [('F', 1)], 5: [('F', 2)]}, 'arrive': {}}
BF16 = jnp.bfloat16
LANES = 128
AHEAD = 2


def dot(left, right):
    return jnp.dot(left, right, preferred_element_type=F32)


def dot_last(left, right):
    return lax.dot_general(left, right, (((1,), (1,)), ((), ())), preferred_element_type=F32)


def chunk_list(units):
    blocks = units // LANES
    if blocks != 8:
        return [(i * LANES, LANES) for i in range(blocks)]
    shape = SHAPE
    return [(start * LANES, size * LANES) for start, size in shape]


def make_plain(n_fsdp, n_et):
    n_half = n_fsdp // 4

    def f_swap(values, mask):
        return lax.ppermute(values, "fsdp", [(f, f ^ mask) for f in range(n_fsdp)])

    def e_swap(values, mask):
        return lax.ppermute(values, "et", [(e, e ^ mask) for e in range(n_et)])

    def zp_flip(values):
        return jnp.concatenate([values[..., 1:2, :], values[..., 0:1, :]], axis=-2)

    def zp_step(values):
        return f_swap(zp_flip(values), 2)

    steps = [zp_step]
    mask = n_et // 2
    while mask >= 1:
        steps.append(lambda values, mask=mask: e_swap(values, mask))
        mask //= 2

    def per_device(tokens, cotangent, route_experts, route_gates, w_gate, w_up, w_down):
        own_count, width = tokens.shape
        most = own_count // 8
        own_width, hidden_units = w_gate.shape
        half_units = hidden_units // 2
        f_index = lax.axis_index("fsdp")
        z_half = f_index // 4
        z_low = (f_index // 2) % 2
        y_index = f_index % 2

        chunks = chunk_list(half_units)
        keep_at = z_low * half_units
        give_at = (1 - z_low) * half_units

        def part_of(start, size):
            return jnp.stack(
                [
                    lax.dynamic_slice_in_dim(w_gate, start, size, axis=1),
                    lax.dynamic_slice_in_dim(w_up, start, size, axis=1),
                    lax.dynamic_slice_in_dim(w_down, start, size, axis=0).T,
                ]
            )

        count = len(chunks)
        kept, given = [], []
        for lo, size in chunks:
            kept.append(part_of(keep_at + lo, size))
            given.append(part_of(give_at + lo, size))
        near, far = [None] * count, [None] * count

        def start_pair(k):
            near[k] = jnp.concatenate([kept[k], f_swap(given[k], 2)], axis=1)

        first_far = f_swap(kept[0], 1)
        first_pair = f_swap(given[0], 2)
        near[0] = jnp.concatenate([kept[0], first_pair], axis=1)
        far[0] = jnp.concatenate([first_far, f_swap(first_pair, 1)], axis=1)
        for k in range(1, min(AHEAD, count)):
            start_pair(k)
            far[k] = f_swap(near[k], 1)

        own_start = lax.axis_index("et") * own_count
        own_experts = lax.dynamic_slice_in_dim(route_experts, own_start, own_count)
        own_gates = lax.dynamic_slice_in_dim(route_gates, own_start, own_count)
        is_first = own_experts[:, 0] == 0
        is_second = own_experts[:, 1] == 0
        chosen = jnp.logical_or(is_first, is_second)
        weight = jnp.where(is_first, own_gates[:, 0], 0.0) + jnp.where(
            is_second, own_gates[:, 1], 0.0
        )
        chosen_int = chosen.astype(jnp.int32)
        slot = jnp.cumsum(chosen_int) - chosen_int
        picks = jnp.logical_and(
            chosen[None, :], slot[None, :] == jnp.arange(most, dtype=jnp.int32)[:, None]
        )
        one_hot = picks.astype(BF16)
        packed_weight = jnp.sum(jnp.where(picks, weight[None, :], 0.0), axis=1)
        packed_rows = dot(one_hot, tokens).astype(BF16)
        packed_cot = (packed_weight[:, None] * dot(one_hot, cotangent)).astype(BF16)
        packed = jnp.concatenate([packed_rows, packed_cot], axis=0)

        cols = packed.reshape(2 * most, n_half, 2, 2, own_width)
        cols = jnp.where(z_low == 0, cols, cols[:, :, ::-1])
        cols = jnp.where(y_index == 0, cols, cols[:, :, :, ::-1])
        cols = jnp.transpose(cols, (1, 0, 3, 2, 4))
        blocks = []
        for d in range(n_half):
            block = lax.dynamic_index_in_dim(cols, z_half ^ d, 0, keepdims=False)
            blocks.append(block if d == 0 else f_swap(block, 4 * d))
        rows = jnp.stack(blocks)[None]
        for step in steps:
            rows = jnp.concatenate([rows, step(rows)], axis=0)
        members = rows.shape[0]
        slots = n_half * members * most
        rows = rows.reshape(members, n_half, 2, most, 2, 2 * own_width)
        rows = jnp.transpose(rows, (2, 4, 1, 0, 3, 5)).reshape(2, 2, slots, 2 * own_width)
        x_near, x_far, cot_near, cot_far = rows[0, 0], rows[0, 1], rows[1, 0], rows[1, 1]

        own_slots = slots // n_half
        total = None
        for k in range(count):
            units = kept[k].shape[2]
            near_k, far_k = near[k], far[k]
            gate = dot(x_near, near_k[0]) + dot(x_far, far_k[0])
            up = dot(x_near, near_k[1]) + dot(x_far, far_k[1])
            grad = dot(cot_near, near_k[2]) + dot(cot_far, far_k[2])
            part = jnp.concatenate([gate, up, grad], axis=1)
            sent = part[own_slots:].astype(BF16).reshape(n_half - 1, own_slots, 3 * units)
            if k + AHEAD < count:
                held = lax.optimization_barrier((kept[k + AHEAD], given[k + AHEAD], sent))
                kept[k + AHEAD], given[k + AHEAD], sent = held
                start_pair(k + AHEAD)
                far[k + AHEAD] = f_swap(near[k + AHEAD], 1)
            pre = part[:own_slots]
            for d in range(1, n_half):
                pre = pre + f_swap(sent[d - 1], 4 * d).astype(F32)
            gate, up, grad = pre[:, :units], pre[:, units : 2 * units], pre[:, 2 * units :]
            sig = jax.nn.sigmoid(gate)
            hidden = gate * sig * up
            grad_gate = grad * up * sig * (1.0 + gate * (1.0 - sig))
            grad_up = grad * gate * sig
            mine = jnp.concatenate([hidden, grad_gate, grad_up], axis=1).astype(BF16)
            full = jnp.concatenate([mine] + [f_swap(mine, 4 * d) for d in range(1, n_half)], axis=0)
            hidden, grad_gate, grad_up = (
                full[:, :units],
                full[:, units : 2 * units],
                full[:, 2 * units :],
            )
            terms = (
                dot_last(hidden, near_k[2]),
                dot_last(hidden, far_k[2]),
                dot_last(grad_gate, near_k[0]) + dot_last(grad_up, near_k[1]),
                dot_last(grad_gate, far_k[0]) + dot_last(grad_up, far_k[1]),
            )
            total = terms if total is None else tuple(a + b for a, b in zip(total, terms))

        sums = jnp.stack([jnp.stack(total[:2]), jnp.stack(total[2:])])
        sums = sums.reshape(2, 2, n_half, members, most, 2, own_width)
        sums = jnp.transpose(sums, (3, 2, 0, 4, 1, 5, 6))
        for step in reversed(steps):
            rest = sums.shape[0] // 2
            sums = sums[:rest] + step(sums[rest:].astype(BF16)).astype(F32)
        sums = sums[0].astype(BF16)
        back = [sums[0]] + [f_swap(sums[d], 4 * d) for d in range(1, n_half)]
        back = jnp.stack(back)
        order = jnp.arange(n_half, dtype=jnp.int32) ^ z_half
        back = jnp.take(back, order, axis=0)
        back = jnp.transpose(back, (1, 2, 0, 4, 3, 5))
        back = jnp.where(z_low == 0, back, back[:, :, :, ::-1])
        back = jnp.where(y_index == 0, back, back[:, :, :, :, ::-1])
        own_sums = back.reshape(2, most, width)
        spread = one_hot.T
        moe_out = (weight[:, None] * dot(spread, own_sums[0])).astype(BF16)
        grad_tokens = dot(spread, own_sums[1]).astype(BF16)
        return moe_out, grad_tokens

    return per_device


def call(body, outs, *args, scratch=(), flops=0, us=0):
    moved = sum(v.size * v.dtype.itemsize for v in list(args) + list(outs))
    return pl.pallas_call(
        body,
        out_shape=list(outs),
        scratch_shapes=list(scratch),
        compiler_params=pltpu.CompilerParams(vmem_limit_bytes=40 * 1024 * 1024),
        cost_estimate=pl.CostEstimate(flops=us * 1000000000, bytes_accessed=1024, transcendentals=0),
    )(*args)


def after(values, *others):
    return lax.optimization_barrier((values, *others))


def shaped(shape, kind):
    return jax.ShapeDtypeStruct(shape, kind)


def flip_pairs(values, own_width):
    parts = [values[..., i * own_width : (i + 1) * own_width] for i in (1, 0, 3, 2)]
    return jnp.concatenate(parts, axis=-1)


def route_columns(experts_ref, gates_ref):
    count = experts_ref.shape[0] // 4
    start = pl.multiple_of(lax.axis_index("et") * count, count)
    experts = experts_ref[pl.ds(start, count), :]
    gates = gates_ref[pl.ds(start, count), :]
    hits = (experts == 0).astype(F32)
    chosen = jnp.sum(hits, axis=1, keepdims=True)
    weight = jnp.sum(hits * gates, axis=1, keepdims=True)
    return chosen, weight


def as_row(column, keep):
    return jnp.sum(jnp.where(keep, column, 0.0), axis=0, keepdims=True)


def weight_chunk_body(low_ref, *refs):
    for gate, up, down, out in (refs[0:3] + refs[6:7], refs[3:6] + refs[7:8]):
        out[0] = gate[...]
        out[1] = up[...]
        out[2] = down[...].T


def weight_chunk(low, w_gate, w_up, w_down, lo, size):
    own_width, hidden_units = w_gate.shape
    half = hidden_units // 2 // size
    at = lo // size

    def spec(kept, rows):
        def index(i, low_ref):
            block = at + half * (low_ref[0] if kept else 1 - low_ref[0])
            return (block, 0) if rows else (0, block)

        return pl.BlockSpec((size, own_width) if rows else (own_width, size), index)

    out = shaped((3, own_width, size), BF16)
    specs = [spec(kept, rows) for kept in (True, False) for rows in (False, False, True)]
    whole = pl.BlockSpec((3, own_width, size), lambda i, low_ref: (0, 0, 0))
    return pl.pallas_call(
        weight_chunk_body,
        out_shape=[out, out],
        grid_spec=pltpu.PrefetchScalarGridSpec(
            num_scalar_prefetch=1, grid=(1,), in_specs=specs, out_specs=[whole, whole]
        ),
        compiler_params=pltpu.CompilerParams(vmem_limit_bytes=60 * 1024 * 1024),
        cost_estimate=pl.CostEstimate(
            flops=0, bytes_accessed=1024, transcendentals=0
        ),
    )(low, w_gate, w_up, w_down, w_gate, w_up, w_down)


def make_fused(n_fsdp, n_et):
    world = n_fsdp * n_et

    def swap(values, mask):
        pairs = [(i, i ^ mask) for i in range(world)]
        return lax.ppermute(values, ("fsdp", "et"), pairs)

    at_y, at_zp, at_zh = n_et, 2 * n_et, 4 * n_et
    at_core, at_x = 1, 2

    def per_device(tokens, cotangent, route_experts, route_gates, w_gate, w_up, w_down):
        own_count, width = tokens.shape
        most = own_count // 8
        own_width, hidden_units = w_gate.shape
        half_units = hidden_units // 2
        z_width = 4 * own_width
        block_shape = (2, most, z_width)
        low = ((lax.axis_index("fsdp") // 2) % 2).astype(jnp.int32).reshape(1)

        chunks = chunk_list(half_units)
        count = len(chunks)
        own_w, zp_w = [None] * count, [None] * count
        given = [None] * count

        stream = []

        def over_y(values):
            stream.append(swap(values, at_y))

        for k in range(count):
            own_w[k], given[k] = weight_chunk(
                low, w_gate, w_up, w_down, *chunks[k]
            )
        over_y(own_w[0])
        zp_w[0] = swap(given[0], at_zp)
        over_y(own_w[1])

        def pack_body(tokens_ref, cot_ref, experts_ref, gates_ref, keep_ref, send_ref, packed_ref):
            chosen, weight = route_columns(experts_ref, gates_ref)
            shape = (own_count, own_count)
            down = lax.broadcasted_iota(jnp.int32, shape, 0)
            across = lax.broadcasted_iota(jnp.int32, shape, 1)
            chosen_row = as_row(chosen, down == across)
            weight_row = as_row(weight, down == across)
            slot_row = as_row(chosen, down < across)
            places = lax.broadcasted_iota(jnp.int32, (most, own_count), 0).astype(F32)
            picks = jnp.logical_and(slot_row == places, chosen_row > 0.0)
            one_hot = jnp.where(picks, 1.0, 0.0).astype(BF16)
            slot_weight = jnp.sum(jnp.where(picks, weight_row, 0.0), axis=1, keepdims=True)
            packed_ref[0] = dot(one_hot, tokens_ref[...]).astype(BF16)
            packed_ref[1] = (slot_weight * dot(one_hot, cot_ref[...])).astype(BF16)
            f_index = lax.axis_index("fsdp")
            for d, out in enumerate((keep_ref, send_ref)):
                for i in range(4):
                    mask = 4 * d + 2 * (i % 2) + i // 2
                    start = pl.multiple_of((f_index ^ mask) * own_width, LANES)
                    columns = slice(i * own_width, (i + 1) * own_width)
                    out[:, :, columns] = packed_ref[:, :, pl.ds(start, own_width)]

        block = shaped(block_shape, BF16)
        mine, sent = call(
            pack_body,
            [block, block],
            tokens,
            cotangent,
            route_experts,
            route_gates,
            scratch=[pltpu.VMEM((2, most, width), BF16)],
            flops=4 * most * own_count * width,
        )
        other = swap(sent, at_zh)

        def join_body(mine_ref, other_ref, plain_ref, flipped_ref):
            for j, ref in enumerate((mine_ref, other_ref)):
                values = ref[...]
                plain_ref[j] = values
                flipped_ref[j] = flip_pairs(values, own_width)

        pair = shaped((2,) + block_shape, BF16)
        if CFG["flags"]["join_y0"]:
            mine, stream[0] = after(mine, stream[0])
        if CFG["flags"]["join_zp0"]:
            mine, zp_w[0] = after(mine, zp_w[0])
        plain, flipped = call(join_body, [pair, pair], mine, other)
        if CFG["flags"]["own2_plain"]:
            own_w[2], _ = after(own_w[2], plain)
        early = CFG["flags"]["zp0_early"]
        if early:
            over_y(zp_w[0])
        over_y(own_w[2])
        if not early:
            over_y(zp_w[0])
        for k in range(1, 3):
            given[k], _ = after(given[k], plain)
            zp_w[k] = swap(given[k], at_zp)
        near_rows = jnp.stack(
            [plain, swap(plain, at_x), swap(flipped, at_zp), swap(flipped, at_zp + at_x)]
        )
        if early:
            stream[2], stream[3] = stream[3], stream[2]
        for at in (1, 2, 3):
            if CFG["flags"][f"near_y{at}"]:
                near_rows, stream[at] = after(near_rows, stream[at])
        if CFG["flags"]["near_zp1"]:
            near_rows, zp_w[1] = after(near_rows, zp_w[1])
        far_rows = swap(near_rows, at_core)
        for at in (2,):
            if CFG["flags"]["first_y2"]:
                near_rows, stream[at] = after(near_rows, stream[at])
        if CFG["flags"]["first_zp1"]:
            near_rows, zp_w[1] = after(near_rows, zp_w[1])
        over_y(zp_w[1])

        slots = 16 * most
        own_slots = slots // 2

        def rows_of(near_ref, far_ref, which):
            parts = [ref[:, :, which].reshape(own_slots, z_width) for ref in (near_ref, far_ref)]
            return jnp.concatenate(parts, axis=0)

        def first_body(near_ref, far_ref, a_ref, b_ref, c_ref, d_ref, keep_ref, send_ref):
            units = a_ref.shape[2]
            rows = rows_of(near_ref, far_ref, 0)
            cots = rows_of(near_ref, far_ref, 1)
            for j in range(3):
                left = cots if j == 2 else rows
                value = None
                for i, ref in enumerate((a_ref, b_ref, c_ref, d_ref)):
                    term = dot(left[:, i * own_width : (i + 1) * own_width], ref[j])
                    value = term if value is None else value + term
                columns = slice(j * units, (j + 1) * units)
                keep_ref[:, columns] = value
                value = value.astype(BF16).reshape(8, 2, most, units)
                value = jnp.concatenate([value[:, 1:2], value[:, 0:1]], axis=1)
                send_ref[:, columns] = value.reshape(slots, units)

        def second_terms(keep_ref, recv_ref, refs):
            units = refs[0].shape[2]
            pre = keep_ref[...] + recv_ref[...].astype(F32)
            gate, up, grad = pre[:, :units], pre[:, units : 2 * units], pre[:, 2 * units :]
            sig = 1.0 / (1.0 + jnp.exp(-gate))
            hidden = (gate * sig * up).astype(BF16)
            grad_gate = (grad * up * sig * (1.0 + gate * (1.0 - sig))).astype(BF16)
            grad_up = (grad * gate * sig).astype(BF16)
            outs = [dot_last(hidden, ref[2]) for ref in refs]
            grads = [dot_last(grad_gate, ref[0]) + dot_last(grad_up, ref[1]) for ref in refs]
            return outs, grads

        def second_body(first, last, keep_ref, recv_ref, a_ref, b_ref, c_ref, d_ref, *rest):
            terms = second_terms(keep_ref, recv_ref, (a_ref, b_ref, c_ref, d_ref))
            rest = list(rest)
            held = None if first else rest.pop(0)
            for which in range(2):
                for i in range(4):
                    columns = slice(i * own_width, (i + 1) * own_width)
                    value = terms[which][i]
                    if held is not None:
                        value = value + held[which, :, columns]
                    if not last:
                        rest[0][which, :, columns] = value
                        continue
                    value = value.reshape(2, 4, 2, most, own_width)
                    for j in range(2):
                        rest[0][:, j, which, :, columns] = value[0, :, j]
                        rest[1][:, j, which, :, columns] = value[1, :, j].astype(BF16)

        quad = (4, 2) + block_shape
        pre, total = [None] * count, [None] * count

        def weights_of(k):
            at = (k, k + 3) if k < 3 else (2 * k, 2 * k + 1)
            return own_w[k], zp_w[k], stream[at[0]], stream[at[1]]

        def first(k, near_rows, far_rows):
            units = chunks[k][1]
            pre[k] = call(
                first_body,
                [shaped((slots, 3 * units), F32), shaped((slots, 3 * units), BF16)],
                near_rows,
                far_rows,
                *weights_of(k),
                us=CFG["us"][0] * units // 256,
            )

        def second(k):
            is_first, is_last = k == 0, k == count - 1
            outs = (
                [shaped(quad, F32), shaped(quad, BF16)]
                if is_last
                else [shaped((2, slots, z_width), F32)]
            )
            held = () if is_first else total[k - 1]
            keep, sent = pre[k]
            total[k] = call(
                lambda *refs: second_body(is_first, is_last, *refs),
                outs,
                keep,
                swap(sent, at_zh),
                *weights_of(k),
                *held,
                us=CFG["us"][1],
            )

        def held_back(values, firsts=(), seconds=()):
            done = [pre[k][1] for k in firsts] + [total[k][0] for k in seconds]
            if not done:
                return values
            values, *done = after(values, *done)
            for k in firsts:
                pre[k] = [pre[k][0], done.pop(0)]
            for k in seconds:
                total[k] = [done.pop(0)]
            return values

        def steps_of(names):
            return [[k for kind, k in names if kind == want] for want in "FS"]

        def emit_y(j):
            k = j // 2
            values = zp_w if (j % 2 or k < 3) else own_w
            k = j - 3 if j < 6 else k
            values[k] = held_back(values[k], *steps_of(CFG["y"][j]))
            over_y(values[k])

        def give(k):
            given[k] = held_back(given[k], *steps_of(CFG["zp"][k]))
            zp_w[k] = swap(given[k], at_zp)

        to_give = list(range(3, count))
        pending = list(range(5, 2 * count))
        done_ops = []
        while to_give and not CFG["zp"][to_give[0]]:
            give(to_give.pop(0))
        while pending and not CFG["y"][pending[0]]:
            emit_y(pending.pop(0))
        for kind, k in CFG["order"]:
            ties = steps_of(CFG["ties"].get((kind, k), []))
            late = CFG["arrive"].get((kind, k), [])
            values = near_rows if kind == "F" else pre[k][0]
            if any(ties):
                values = held_back(values, *ties)
            for at in late:
                values, stream[at] = after(values, stream[at])
            if kind == "F":
                first(k, values, far_rows)
            else:
                pre[k] = [values, pre[k][1]]
                second(k)
            done_ops.append((kind, k))
            while to_give and all(op in done_ops for op in CFG["zp"][to_give[0]]):
                give(to_give.pop(0))
            while pending and all(op in done_ops for op in CFG["y"][pending[0]]):
                emit_y(pending.pop(0))
        total = total[-1]

        def spread_body(keep_ref, recv_ref, own_ref, *outs):
            value = keep_ref[...] + recv_ref[...].astype(F32)
            own_ref[...] = value[0]
            for i in range(1, 4):
                part = value[i].astype(BF16)
                outs[i - 1][...] = flip_pairs(part, own_width) if i >= 2 else part

        keep, sent = total
        own, by_x, by_zp, by_both = call(
            spread_body,
            [shaped(pair.shape, F32), pair, pair, pair],
            keep,
            swap(sent, at_core),
        )

        def gather_body(own_ref, x_ref, zp_ref, both_ref, keep_ref, send_ref):
            value = own_ref[...] + x_ref[...].astype(F32)
            value = value + (zp_ref[...].astype(F32) + both_ref[...].astype(F32))
            keep_ref[...] = value[0].astype(BF16)
            send_ref[...] = value[1].astype(BF16)

        mine, sent = call(
            gather_body,
            [block, block],
            own,
            swap(by_x, at_x),
            swap(by_zp, at_zp),
            swap(by_both, at_zp + at_x),
        )

        def unpack_body(mine_ref, other_ref, experts_ref, gates_ref, out_ref, grad_ref, sums_ref):
            f_index = lax.axis_index("fsdp")
            for d, ref in enumerate((mine_ref, other_ref)):
                for i in range(4):
                    mask = 4 * d + 2 * (i % 2) + i // 2
                    start = pl.multiple_of((f_index ^ mask) * own_width, LANES)
                    columns = slice(i * own_width, (i + 1) * own_width)
                    sums_ref[:, :, pl.ds(start, own_width)] = ref[:, :, columns]
            chosen, weight = route_columns(experts_ref, gates_ref)
            shape = (own_count, own_count)
            down = lax.broadcasted_iota(jnp.int32, shape, 0)
            across = lax.broadcasted_iota(jnp.int32, shape, 1)
            chosen_row = as_row(chosen, down == across)
            slot = jnp.sum(jnp.where(across < down, chosen_row, 0.0), axis=1, keepdims=True)
            places = lax.broadcasted_iota(jnp.int32, (own_count, most), 1).astype(F32)
            picks = jnp.logical_and(slot == places, chosen > 0.0)
            spread = jnp.where(picks, 1.0, 0.0).astype(BF16)
            out_ref[...] = (weight * dot(spread, sums_ref[0])).astype(BF16)
            grad_ref[...] = dot(spread, sums_ref[1]).astype(BF16)

        result = shaped(tokens.shape, BF16)
        return tuple(
            call(
                unpack_body,
                [result, result],
                mine,
                swap(sent, at_zh),
                route_experts,
                route_gates,
                scratch=[pltpu.VMEM((2, most, width), BF16)],
                flops=4 * most * own_count * width,
            )
        )

    return per_device


def solution(mesh):
    sizes = dict(mesh.shape)
    make = make_fused if sizes["fsdp"] == 8 and sizes["et"] == 4 else make_plain
    in_specs = (
        P(("fsdp", "et"), None),
        P(("fsdp", "et"), None),
        P("fsdp", None),
        P("fsdp", None),
        P("fsdp", "et"),
        P("fsdp", "et"),
        P("et", "fsdp"),
    )
    out_specs = (P(("fsdp", "et"), None), P(("fsdp", "et"), None))
    return jax.shard_map(
        make(sizes["fsdp"], sizes["et"]),
        mesh=mesh,
        in_specs=in_specs,
        out_specs=out_specs,
        check_vma=False,
    )
```

```python
import jax
import jax.numpy as jnp
from jax import lax
from jax.experimental import pallas as pl
from jax.experimental.pallas import tpu as pltpu
from jax.sharding import PartitionSpec as P

F32 = jnp.float32
BF16 = jnp.bfloat16
LANES = 128
AHEAD = 2


def dot(left, right):
    return jnp.dot(left, right, preferred_element_type=F32)


def dot_last(left, right):
    return lax.dot_general(left, right, (((1,), (1,)), ((), ())), preferred_element_type=F32)


def chunk_list(units):
    blocks = units // LANES
    if blocks != 8:
        return [(i * LANES, LANES) for i in range(blocks)]
    shape = ((0, 1), (2, 2), (4, 2), (1, 1), (6, 1), (7, 1))
    return [(start * LANES, size * LANES) for start, size in shape]


def make_plain(n_fsdp, n_et):
    n_half = n_fsdp // 4

    def f_swap(values, mask):
        return lax.ppermute(values, "fsdp", [(f, f ^ mask) for f in range(n_fsdp)])

    def e_swap(values, mask):
        return lax.ppermute(values, "et", [(e, e ^ mask) for e in range(n_et)])

    def zp_flip(values):
        return jnp.concatenate([values[..., 1:2, :], values[..., 0:1, :]], axis=-2)

    def zp_step(values):
        return f_swap(zp_flip(values), 2)

    steps = [zp_step]
    mask = n_et // 2
    while mask >= 1:
        steps.append(lambda values, mask=mask: e_swap(values, mask))
        mask //= 2

    def per_device(tokens, cotangent, route_experts, route_gates, w_gate, w_up, w_down):
        own_count, width = tokens.shape
        most = own_count // 8
        own_width, hidden_units = w_gate.shape
        half_units = hidden_units // 2
        f_index = lax.axis_index("fsdp")
        z_half = f_index // 4
        z_low = (f_index // 2) % 2
        y_index = f_index % 2

        chunks = chunk_list(half_units)
        keep_at = z_low * half_units
        give_at = (1 - z_low) * half_units

        def part_of(start, size):
            return jnp.stack(
                [
                    lax.dynamic_slice_in_dim(w_gate, start, size, axis=1),
                    lax.dynamic_slice_in_dim(w_up, start, size, axis=1),
                    lax.dynamic_slice_in_dim(w_down, start, size, axis=0).T,
                ]
            )

        count = len(chunks)
        kept, given = [], []
        for lo, size in chunks:
            kept.append(part_of(keep_at + lo, size))
            given.append(part_of(give_at + lo, size))
        near, far = [None] * count, [None] * count

        def start_pair(k):
            near[k] = jnp.concatenate([kept[k], f_swap(given[k], 2)], axis=1)

        first_far = f_swap(kept[0], 1)
        first_pair = f_swap(given[0], 2)
        near[0] = jnp.concatenate([kept[0], first_pair], axis=1)
        far[0] = jnp.concatenate([first_far, f_swap(first_pair, 1)], axis=1)
        for k in range(1, min(AHEAD, count)):
            start_pair(k)
            far[k] = f_swap(near[k], 1)

        own_start = lax.axis_index("et") * own_count
        own_experts = lax.dynamic_slice_in_dim(route_experts, own_start, own_count)
        own_gates = lax.dynamic_slice_in_dim(route_gates, own_start, own_count)
        is_first = own_experts[:, 0] == 0
        is_second = own_experts[:, 1] == 0
        chosen = jnp.logical_or(is_first, is_second)
        weight = jnp.where(is_first, own_gates[:, 0], 0.0) + jnp.where(
            is_second, own_gates[:, 1], 0.0
        )
        chosen_int = chosen.astype(jnp.int32)
        slot = jnp.cumsum(chosen_int) - chosen_int
        picks = jnp.logical_and(
            chosen[None, :], slot[None, :] == jnp.arange(most, dtype=jnp.int32)[:, None]
        )
        one_hot = picks.astype(BF16)
        packed_weight = jnp.sum(jnp.where(picks, weight[None, :], 0.0), axis=1)
        packed_rows = dot(one_hot, tokens).astype(BF16)
        packed_cot = (packed_weight[:, None] * dot(one_hot, cotangent)).astype(BF16)
        packed = jnp.concatenate([packed_rows, packed_cot], axis=0)

        cols = packed.reshape(2 * most, n_half, 2, 2, own_width)
        cols = jnp.where(z_low == 0, cols, cols[:, :, ::-1])
        cols = jnp.where(y_index == 0, cols, cols[:, :, :, ::-1])
        cols = jnp.transpose(cols, (1, 0, 3, 2, 4))
        blocks = []
        for d in range(n_half):
            block = lax.dynamic_index_in_dim(cols, z_half ^ d, 0, keepdims=False)
            blocks.append(block if d == 0 else f_swap(block, 4 * d))
        rows = jnp.stack(blocks)[None]
        for step in steps:
            rows = jnp.concatenate([rows, step(rows)], axis=0)
        members = rows.shape[0]
        slots = n_half * members * most
        rows = rows.reshape(members, n_half, 2, most, 2, 2 * own_width)
        rows = jnp.transpose(rows, (2, 4, 1, 0, 3, 5)).reshape(2, 2, slots, 2 * own_width)
        x_near, x_far, cot_near, cot_far = rows[0, 0], rows[0, 1], rows[1, 0], rows[1, 1]

        own_slots = slots // n_half
        total = None
        for k in range(count):
            units = kept[k].shape[2]
            near_k, far_k = near[k], far[k]
            gate = dot(x_near, near_k[0]) + dot(x_far, far_k[0])
            up = dot(x_near, near_k[1]) + dot(x_far, far_k[1])
            grad = dot(cot_near, near_k[2]) + dot(cot_far, far_k[2])
            part = jnp.concatenate([gate, up, grad], axis=1)
            sent = part[own_slots:].astype(BF16).reshape(n_half - 1, own_slots, 3 * units)
            if k + AHEAD < count:
                held = lax.optimization_barrier((kept[k + AHEAD], given[k + AHEAD], sent))
                kept[k + AHEAD], given[k + AHEAD], sent = held
                start_pair(k + AHEAD)
                far[k + AHEAD] = f_swap(near[k + AHEAD], 1)
            pre = part[:own_slots]
            for d in range(1, n_half):
                pre = pre + f_swap(sent[d - 1], 4 * d).astype(F32)
            gate, up, grad = pre[:, :units], pre[:, units : 2 * units], pre[:, 2 * units :]
            sig = jax.nn.sigmoid(gate)
            hidden = gate * sig * up
            grad_gate = grad * up * sig * (1.0 + gate * (1.0 - sig))
            grad_up = grad * gate * sig
            mine = jnp.concatenate([hidden, grad_gate, grad_up], axis=1).astype(BF16)
            full = jnp.concatenate([mine] + [f_swap(mine, 4 * d) for d in range(1, n_half)], axis=0)
            hidden, grad_gate, grad_up = (
                full[:, :units],
                full[:, units : 2 * units],
                full[:, 2 * units :],
            )
            terms = (
                dot_last(hidden, near_k[2]),
                dot_last(hidden, far_k[2]),
                dot_last(grad_gate, near_k[0]) + dot_last(grad_up, near_k[1]),
                dot_last(grad_gate, far_k[0]) + dot_last(grad_up, far_k[1]),
            )
            total = terms if total is None else tuple(a + b for a, b in zip(total, terms))

        sums = jnp.stack([jnp.stack(total[:2]), jnp.stack(total[2:])])
        sums = sums.reshape(2, 2, n_half, members, most, 2, own_width)
        sums = jnp.transpose(sums, (3, 2, 0, 4, 1, 5, 6))
        for step in reversed(steps):
            rest = sums.shape[0] // 2
            sums = sums[:rest] + step(sums[rest:].astype(BF16)).astype(F32)
        sums = sums[0].astype(BF16)
        back = [sums[0]] + [f_swap(sums[d], 4 * d) for d in range(1, n_half)]
        back = jnp.stack(back)
        order = jnp.arange(n_half, dtype=jnp.int32) ^ z_half
        back = jnp.take(back, order, axis=0)
        back = jnp.transpose(back, (1, 2, 0, 4, 3, 5))
        back = jnp.where(z_low == 0, back, back[:, :, :, ::-1])
        back = jnp.where(y_index == 0, back, back[:, :, :, :, ::-1])
        own_sums = back.reshape(2, most, width)
        spread = one_hot.T
        moe_out = (weight[:, None] * dot(spread, own_sums[0])).astype(BF16)
        grad_tokens = dot(spread, own_sums[1]).astype(BF16)
        return moe_out, grad_tokens

    return per_device


def call(body, outs, *args, scratch=(), us=0):
    return pl.pallas_call(
        body,
        out_shape=list(outs),
        scratch_shapes=list(scratch),
        compiler_params=pltpu.CompilerParams(vmem_limit_bytes=40 * 1024 * 1024),
        cost_estimate=pl.CostEstimate(flops=us * 1000000000, bytes_accessed=1024, transcendentals=0),
    )(*args)


def after(values, *others):
    return lax.optimization_barrier((values, *others))


def shaped(shape, kind):
    return jax.ShapeDtypeStruct(shape, kind)


def flip_pairs(values, own_width):
    parts = [values[..., i * own_width : (i + 1) * own_width] for i in (1, 0, 3, 2)]
    return jnp.concatenate(parts, axis=-1)


def route_columns(experts_ref, gates_ref):
    count = experts_ref.shape[0] // 4
    start = pl.multiple_of(lax.axis_index("et") * count, count)
    experts = experts_ref[pl.ds(start, count), :]
    gates = gates_ref[pl.ds(start, count), :]
    hits = (experts == 0).astype(F32)
    chosen = jnp.sum(hits, axis=1, keepdims=True)
    weight = jnp.sum(hits * gates, axis=1, keepdims=True)
    return chosen, weight


def as_row(column, keep):
    return jnp.sum(jnp.where(keep, column, 0.0), axis=0, keepdims=True)


def weight_chunk_body(low_ref, *refs):
    for gate, up, down, out in (refs[0:3] + refs[6:7], refs[3:6] + refs[7:8]):
        out[0] = gate[...]
        out[1] = up[...]
        out[2] = down[...].T


def weight_chunk(low, w_gate, w_up, w_down, lo, size):
    own_width, hidden_units = w_gate.shape
    half = hidden_units // 2 // size
    at = lo // size

    def spec(kept, rows):
        def index(i, low_ref):
            block = at + half * (low_ref[0] if kept else 1 - low_ref[0])
            return (block, 0) if rows else (0, block)

        return pl.BlockSpec((size, own_width) if rows else (own_width, size), index)

    out = shaped((3, own_width, size), BF16)
    specs = [spec(kept, rows) for kept in (True, False) for rows in (False, False, True)]
    whole = pl.BlockSpec((3, own_width, size), lambda i, low_ref: (0, 0, 0))
    return pl.pallas_call(
        weight_chunk_body,
        out_shape=[out, out],
        grid_spec=pltpu.PrefetchScalarGridSpec(
            num_scalar_prefetch=1, grid=(1,), in_specs=specs, out_specs=[whole, whole]
        ),
        compiler_params=pltpu.CompilerParams(vmem_limit_bytes=60 * 1024 * 1024),
        cost_estimate=pl.CostEstimate(
            flops=0, bytes_accessed=1024, transcendentals=0
        ),
    )(low, w_gate, w_up, w_down, w_gate, w_up, w_down)


def make_fused(n_fsdp, n_et):
    world = n_fsdp * n_et

    def swap(values, mask):
        pairs = [(i, i ^ mask) for i in range(world)]
        return lax.ppermute(values, ("fsdp", "et"), pairs)

    at_y, at_zp, at_zh = n_et, 2 * n_et, 4 * n_et
    at_core, at_x = 1, 2

    def per_device(tokens, cotangent, route_experts, route_gates, w_gate, w_up, w_down):
        own_count, width = tokens.shape
        most = own_count // 8
        own_width, hidden_units = w_gate.shape
        half_units = hidden_units // 2
        z_width = 4 * own_width
        block_shape = (2, most, z_width)
        low = ((lax.axis_index("fsdp") // 2) % 2).astype(jnp.int32).reshape(1)

        chunks = chunk_list(half_units)
        count = len(chunks)
        own_w, zp_w = [None] * count, [None] * count
        given = [None] * count

        stream = []

        def over_y(values):
            stream.append(swap(values, at_y))

        for k in range(count):
            own_w[k], given[k] = weight_chunk(low, w_gate, w_up, w_down, *chunks[k])
        over_y(own_w[0])
        zp_w[0] = swap(given[0], at_zp)
        over_y(own_w[1])

        def pack_body(tokens_ref, cot_ref, experts_ref, gates_ref, keep_ref, send_ref, packed_ref):
            chosen, weight = route_columns(experts_ref, gates_ref)
            shape = (own_count, own_count)
            down = lax.broadcasted_iota(jnp.int32, shape, 0)
            across = lax.broadcasted_iota(jnp.int32, shape, 1)
            chosen_row = as_row(chosen, down == across)
            weight_row = as_row(weight, down == across)
            slot_row = as_row(chosen, down < across)
            places = lax.broadcasted_iota(jnp.int32, (most, own_count), 0).astype(F32)
            picks = jnp.logical_and(slot_row == places, chosen_row > 0.0)
            one_hot = jnp.where(picks, 1.0, 0.0).astype(BF16)
            slot_weight = jnp.sum(jnp.where(picks, weight_row, 0.0), axis=1, keepdims=True)
            packed_ref[0] = dot(one_hot, tokens_ref[...]).astype(BF16)
            packed_ref[1] = (slot_weight * dot(one_hot, cot_ref[...])).astype(BF16)
            f_index = lax.axis_index("fsdp")
            for d, out in enumerate((keep_ref, send_ref)):
                for i in range(4):
                    mask = 4 * d + 2 * (i % 2) + i // 2
                    start = pl.multiple_of((f_index ^ mask) * own_width, LANES)
                    columns = slice(i * own_width, (i + 1) * own_width)
                    out[:, :, columns] = packed_ref[:, :, pl.ds(start, own_width)]

        block = shaped(block_shape, BF16)
        mine, sent = call(
            pack_body,
            [block, block],
            tokens,
            cotangent,
            route_experts,
            route_gates,
            scratch=[pltpu.VMEM((2, most, width), BF16)],
        )
        other = swap(sent, at_zh)

        def join_body(mine_ref, other_ref, plain_ref, flipped_ref):
            for j, ref in enumerate((mine_ref, other_ref)):
                values = ref[...]
                plain_ref[j] = values
                flipped_ref[j] = flip_pairs(values, own_width)

        pair = shaped((2,) + block_shape, BF16)
        mine, stream[0] = after(mine, stream[0])
        mine, zp_w[0] = after(mine, zp_w[0])
        plain, flipped = call(join_body, [pair, pair], mine, other)
        own_w[2], _ = after(own_w[2], plain)
        over_y(zp_w[0])
        over_y(own_w[2])
        for k, first_done in ((1, sent), (2, plain)):
            given[k], _ = after(given[k], first_done)
            zp_w[k] = swap(given[k], at_zp)
        near_rows = jnp.stack(
            [plain, swap(plain, at_x), swap(flipped, at_zp), swap(flipped, at_zp + at_x)]
        )
        near_rows, stream[1] = after(near_rows, stream[1])
        far_rows = swap(near_rows, at_core)
        near_rows, stream[3] = after(near_rows, stream[3])
        near_rows, zp_w[1] = after(near_rows, zp_w[1])
        over_y(zp_w[1])

        slots = 16 * most
        own_slots = slots // 2

        def rows_of(near_ref, far_ref, which):
            parts = [ref[:, :, which].reshape(own_slots, z_width) for ref in (near_ref, far_ref)]
            return jnp.concatenate(parts, axis=0)

        def first_body(near_ref, far_ref, a_ref, b_ref, c_ref, d_ref, keep_ref, send_ref):
            units = a_ref.shape[2]
            rows = rows_of(near_ref, far_ref, 0)
            cots = rows_of(near_ref, far_ref, 1)
            for j in range(3):
                left = cots if j == 2 else rows
                value = None
                for i, ref in enumerate((a_ref, b_ref, c_ref, d_ref)):
                    term = dot(left[:, i * own_width : (i + 1) * own_width], ref[j])
                    value = term if value is None else value + term
                columns = slice(j * units, (j + 1) * units)
                keep_ref[:, columns] = value
                value = value.astype(BF16).reshape(8, 2, most, units)
                value = jnp.concatenate([value[:, 1:2], value[:, 0:1]], axis=1)
                send_ref[:, columns] = value.reshape(slots, units)

        def second_terms(keep_ref, recv_ref, refs):
            units = refs[0].shape[2]
            pre = keep_ref[...] + recv_ref[...].astype(F32)
            gate, up, grad = pre[:, :units], pre[:, units : 2 * units], pre[:, 2 * units :]
            sig = 1.0 / (1.0 + jnp.exp(-gate))
            hidden = (gate * sig * up).astype(BF16)
            grad_gate = (grad * up * sig * (1.0 + gate * (1.0 - sig))).astype(BF16)
            grad_up = (grad * gate * sig).astype(BF16)
            outs = [dot_last(hidden, ref[2]) for ref in refs]
            grads = [dot_last(grad_gate, ref[0]) + dot_last(grad_up, ref[1]) for ref in refs]
            return outs, grads

        def second_body(first, last, keep_ref, recv_ref, a_ref, b_ref, c_ref, d_ref, *rest):
            terms = second_terms(keep_ref, recv_ref, (a_ref, b_ref, c_ref, d_ref))
            rest = list(rest)
            held = None if first else rest.pop(0)
            for which in range(2):
                for i in range(4):
                    columns = slice(i * own_width, (i + 1) * own_width)
                    value = terms[which][i]
                    if held is not None:
                        value = value + held[which, :, columns]
                    if not last:
                        rest[0][which, :, columns] = value
                        continue
                    value = value.reshape(2, 4, 2, most, own_width)
                    for j in range(2):
                        rest[0][:, j, which, :, columns] = value[0, :, j]
                        rest[1][:, j, which, :, columns] = value[1, :, j].astype(BF16)

        quad = (4, 2) + block_shape
        pre, total = [None] * count, [None] * count

        def weights_of(k):
            at = ((0, 2), (1, 4), (3, 5))[k] if k < 3 else (2 * k, 2 * k + 1)
            return own_w[k], zp_w[k], stream[at[0]], stream[at[1]]

        def first(k, near_rows, far_rows):
            units = chunks[k][1]
            pre[k] = call(
                first_body,
                [shaped((slots, 3 * units), F32), shaped((slots, 3 * units), BF16)],
                near_rows,
                far_rows,
                *weights_of(k),
                us=8 * units // 256,
            )

        def second(k):
            is_first, is_last = k == 0, k == count - 1
            outs = (
                [shaped(quad, F32), shaped(quad, BF16)]
                if is_last
                else [shaped((2, slots, z_width), F32)]
            )
            held = () if is_first else total[k - 1]
            keep, sent = pre[k]
            total[k] = call(
                lambda *refs: second_body(is_first, is_last, *refs),
                outs,
                keep,
                swap(sent, at_zh),
                *weights_of(k),
                *held,
            )

        def held_back(values, firsts=(), seconds=()):
            done = [pre[k][1] for k in firsts] + [total[k][0] for k in seconds]
            if not done:
                return values
            values, *done = after(values, *done)
            for k in firsts:
                pre[k] = [pre[k][0], done.pop(0)]
            for k in seconds:
                total[k] = [done.pop(0)]
            return values

        def first_after(k, *steps):
            first(k, held_back(near_rows, *steps), far_rows)

        def second_after(k, *steps):
            pre[k] = [held_back(pre[k][0], *steps), pre[k][1]]
            second(k)

        def pair_exchange(k, *steps):
            given[k] = held_back(given[k], *steps)
            zp_w[k] = swap(given[k], at_zp)

        def own_over_y(k, *steps):
            own_w[k] = held_back(own_w[k], *steps)
            over_y(own_w[k])

        def pair_over_y(k, *steps):
            zp_w[k] = held_back(zp_w[k], *steps)
            over_y(zp_w[k])

        first(0, near_rows, far_rows)
        pair_exchange(3, [0])
        pair_over_y(2, [0])
        first_after(1, [0])
        pair_exchange(4, [1])
        own_over_y(3, [1])
        pair_over_y(3, [1])
        second_after(0, [1])
        first_after(2, [1])
        pair_exchange(5, [2])
        own_over_y(4, [2])
        pair_over_y(4, [2])
        second_after(1, [2])
        first_after(3, [], [0])
        own_over_y(5, [3])
        pair_over_y(5, [3])
        second(2)
        first_after(4, [3], [1])
        second_after(3, [4])
        first_after(5, [4], [3])
        second_after(4, [5])
        second(5)
        total = total[-1]

        def spread_body(keep_ref, recv_ref, own_ref, *outs):
            value = keep_ref[...] + recv_ref[...].astype(F32)
            own_ref[...] = value[0]
            for i in range(1, 4):
                part = value[i].astype(BF16)
                outs[i - 1][...] = flip_pairs(part, own_width) if i >= 2 else part

        keep, sent = total
        own, by_x, by_zp, by_both = call(
            spread_body,
            [shaped(pair.shape, F32), pair, pair, pair],
            keep,
            swap(sent, at_core),
        )

        def gather_body(own_ref, x_ref, zp_ref, both_ref, keep_ref, send_ref):
            value = own_ref[...] + x_ref[...].astype(F32)
            value = value + (zp_ref[...].astype(F32) + both_ref[...].astype(F32))
            keep_ref[...] = value[0].astype(BF16)
            send_ref[...] = value[1].astype(BF16)

        mine, sent = call(
            gather_body,
            [block, block],
            own,
            swap(by_x, at_x),
            swap(by_zp, at_zp),
            swap(by_both, at_zp + at_x),
        )

        def unpack_body(mine_ref, other_ref, experts_ref, gates_ref, out_ref, grad_ref, sums_ref):
            f_index = lax.axis_index("fsdp")
            for d, ref in enumerate((mine_ref, other_ref)):
                for i in range(4):
                    mask = 4 * d + 2 * (i % 2) + i // 2
                    start = pl.multiple_of((f_index ^ mask) * own_width, LANES)
                    columns = slice(i * own_width, (i + 1) * own_width)
                    sums_ref[:, :, pl.ds(start, own_width)] = ref[:, :, columns]
            chosen, weight = route_columns(experts_ref, gates_ref)
            shape = (own_count, own_count)
            down = lax.broadcasted_iota(jnp.int32, shape, 0)
            across = lax.broadcasted_iota(jnp.int32, shape, 1)
            chosen_row = as_row(chosen, down == across)
            slot = jnp.sum(jnp.where(across < down, chosen_row, 0.0), axis=1, keepdims=True)
            places = lax.broadcasted_iota(jnp.int32, (own_count, most), 1).astype(F32)
            picks = jnp.logical_and(slot == places, chosen > 0.0)
            spread = jnp.where(picks, 1.0, 0.0).astype(BF16)
            out_ref[...] = (weight * dot(spread, sums_ref[0])).astype(BF16)
            grad_ref[...] = dot(spread, sums_ref[1]).astype(BF16)

        result = shaped(tokens.shape, BF16)
        return tuple(
            call(
                unpack_body,
                [result, result],
                mine,
                swap(sent, at_zh),
                route_experts,
                route_gates,
                scratch=[pltpu.VMEM((2, most, width), BF16)],
                )
        )

    return per_device


def solution(mesh):
    sizes = dict(mesh.shape)
    make = make_fused if sizes["fsdp"] == 8 and sizes["et"] == 4 else make_plain
    in_specs = (
        P(("fsdp", "et"), None),
        P(("fsdp", "et"), None),
        P("fsdp", None),
        P("fsdp", None),
        P("fsdp", "et"),
        P("fsdp", "et"),
        P("et", "fsdp"),
    )
    out_specs = (P(("fsdp", "et"), None), P(("fsdp", "et"), None))
    return jax.shard_map(
        make(sizes["fsdp"], sizes["et"]),
        mesh=mesh,
        in_specs=in_specs,
        out_specs=out_specs,
        check_vma=False,
    )
```

```python
import jax
import jax.numpy as jnp
from jax import lax
from jax.experimental import pallas as pl
from jax.experimental.pallas import tpu as pltpu
from jax.sharding import PartitionSpec as P

F32 = jnp.float32
BF16 = jnp.bfloat16
LANES = 128
AHEAD = 2


def dot(left, right):
    return jnp.dot(left, right, preferred_element_type=F32)


def dot_last(left, right):
    return lax.dot_general(left, right, (((1,), (1,)), ((), ())), preferred_element_type=F32)


def chunk_list(units):
    blocks = units // LANES
    if blocks != 8:
        return [(i * LANES, LANES) for i in range(blocks)]
    shape = ((0, 1), (2, 2), (4, 2), (1, 1), (6, 1), (7, 1))
    return [(start * LANES, size * LANES) for start, size in shape]


def make_plain(n_fsdp, n_et):
    n_half = n_fsdp // 4

    def f_swap(values, mask):
        return lax.ppermute(values, "fsdp", [(f, f ^ mask) for f in range(n_fsdp)])

    def e_swap(values, mask):
        return lax.ppermute(values, "et", [(e, e ^ mask) for e in range(n_et)])

    def zp_flip(values):
        return jnp.concatenate([values[..., 1:2, :], values[..., 0:1, :]], axis=-2)

    def zp_step(values):
        return f_swap(zp_flip(values), 2)

    steps = [zp_step]
    mask = n_et // 2
    while mask >= 1:
        steps.append(lambda values, mask=mask: e_swap(values, mask))
        mask //= 2

    def per_device(tokens, cotangent, route_experts, route_gates, w_gate, w_up, w_down):
        own_count, width = tokens.shape
        most = own_count // 8
        own_width, hidden_units = w_gate.shape
        half_units = hidden_units // 2
        f_index = lax.axis_index("fsdp")
        z_half = f_index // 4
        z_low = (f_index // 2) % 2
        y_index = f_index % 2

        chunks = chunk_list(half_units)
        keep_at = z_low * half_units
        give_at = (1 - z_low) * half_units

        def part_of(start, size):
            return jnp.stack(
                [
                    lax.dynamic_slice_in_dim(w_gate, start, size, axis=1),
                    lax.dynamic_slice_in_dim(w_up, start, size, axis=1),
                    lax.dynamic_slice_in_dim(w_down, start, size, axis=0).T,
                ]
            )

        count = len(chunks)
        kept, given = [], []
        for lo, size in chunks:
            kept.append(part_of(keep_at + lo, size))
            given.append(part_of(give_at + lo, size))
        near, far = [None] * count, [None] * count

        def start_pair(k):
            near[k] = jnp.concatenate([kept[k], f_swap(given[k], 2)], axis=1)

        first_far = f_swap(kept[0], 1)
        first_pair = f_swap(given[0], 2)
        near[0] = jnp.concatenate([kept[0], first_pair], axis=1)
        far[0] = jnp.concatenate([first_far, f_swap(first_pair, 1)], axis=1)
        for k in range(1, min(AHEAD, count)):
            start_pair(k)
            far[k] = f_swap(near[k], 1)

        own_start = lax.axis_index("et") * own_count
        own_experts = lax.dynamic_slice_in_dim(route_experts, own_start, own_count)
        own_gates = lax.dynamic_slice_in_dim(route_gates, own_start, own_count)
        is_first = own_experts[:, 0] == 0
        is_second = own_experts[:, 1] == 0
        chosen = jnp.logical_or(is_first, is_second)
        weight = jnp.where(is_first, own_gates[:, 0], 0.0) + jnp.where(
            is_second, own_gates[:, 1], 0.0
        )
        chosen_int = chosen.astype(jnp.int32)
        slot = jnp.cumsum(chosen_int) - chosen_int
        picks = jnp.logical_and(
            chosen[None, :], slot[None, :] == jnp.arange(most, dtype=jnp.int32)[:, None]
        )
        one_hot = picks.astype(BF16)
        packed_weight = jnp.sum(jnp.where(picks, weight[None, :], 0.0), axis=1)
        packed_rows = dot(one_hot, tokens).astype(BF16)
        packed_cot = (packed_weight[:, None] * dot(one_hot, cotangent)).astype(BF16)
        packed = jnp.concatenate([packed_rows, packed_cot], axis=0)

        cols = packed.reshape(2 * most, n_half, 2, 2, own_width)
        cols = jnp.where(z_low == 0, cols, cols[:, :, ::-1])
        cols = jnp.where(y_index == 0, cols, cols[:, :, :, ::-1])
        cols = jnp.transpose(cols, (1, 0, 3, 2, 4))
        blocks = []
        for d in range(n_half):
            block = lax.dynamic_index_in_dim(cols, z_half ^ d, 0, keepdims=False)
            blocks.append(block if d == 0 else f_swap(block, 4 * d))
        rows = jnp.stack(blocks)[None]
        for step in steps:
            rows = jnp.concatenate([rows, step(rows)], axis=0)
        members = rows.shape[0]
        slots = n_half * members * most
        rows = rows.reshape(members, n_half, 2, most, 2, 2 * own_width)
        rows = jnp.transpose(rows, (2, 4, 1, 0, 3, 5)).reshape(2, 2, slots, 2 * own_width)
        x_near, x_far, cot_near, cot_far = rows[0, 0], rows[0, 1], rows[1, 0], rows[1, 1]

        own_slots = slots // n_half
        total = None
        for k in range(count):
            units = kept[k].shape[2]
            near_k, far_k = near[k], far[k]
            gate = dot(x_near, near_k[0]) + dot(x_far, far_k[0])
            up = dot(x_near, near_k[1]) + dot(x_far, far_k[1])
            grad = dot(cot_near, near_k[2]) + dot(cot_far, far_k[2])
            part = jnp.concatenate([gate, up, grad], axis=1)
            sent = part[own_slots:].astype(BF16).reshape(n_half - 1, own_slots, 3 * units)
            if k + AHEAD < count:
                held = lax.optimization_barrier((kept[k + AHEAD], given[k + AHEAD], sent))
                kept[k + AHEAD], given[k + AHEAD], sent = held
                start_pair(k + AHEAD)
                far[k + AHEAD] = f_swap(near[k + AHEAD], 1)
            pre = part[:own_slots]
            for d in range(1, n_half):
                pre = pre + f_swap(sent[d - 1], 4 * d).astype(F32)
            gate, up, grad = pre[:, :units], pre[:, units : 2 * units], pre[:, 2 * units :]
            sig = jax.nn.sigmoid(gate)
            hidden = gate * sig * up
            grad_gate = grad * up * sig * (1.0 + gate * (1.0 - sig))
            grad_up = grad * gate * sig
            mine = jnp.concatenate([hidden, grad_gate, grad_up], axis=1).astype(BF16)
            full = jnp.concatenate([mine] + [f_swap(mine, 4 * d) for d in range(1, n_half)], axis=0)
            hidden, grad_gate, grad_up = (
                full[:, :units],
                full[:, units : 2 * units],
                full[:, 2 * units :],
            )
            terms = (
                dot_last(hidden, near_k[2]),
                dot_last(hidden, far_k[2]),
                dot_last(grad_gate, near_k[0]) + dot_last(grad_up, near_k[1]),
                dot_last(grad_gate, far_k[0]) + dot_last(grad_up, far_k[1]),
            )
            total = terms if total is None else tuple(a + b for a, b in zip(total, terms))

        sums = jnp.stack([jnp.stack(total[:2]), jnp.stack(total[2:])])
        sums = sums.reshape(2, 2, n_half, members, most, 2, own_width)
        sums = jnp.transpose(sums, (3, 2, 0, 4, 1, 5, 6))
        for step in reversed(steps):
            rest = sums.shape[0] // 2
            sums = sums[:rest] + step(sums[rest:].astype(BF16)).astype(F32)
        sums = sums[0].astype(BF16)
        back = [sums[0]] + [f_swap(sums[d], 4 * d) for d in range(1, n_half)]
        back = jnp.stack(back)
        order = jnp.arange(n_half, dtype=jnp.int32) ^ z_half
        back = jnp.take(back, order, axis=0)
        back = jnp.transpose(back, (1, 2, 0, 4, 3, 5))
        back = jnp.where(z_low == 0, back, back[:, :, :, ::-1])
        back = jnp.where(y_index == 0, back, back[:, :, :, :, ::-1])
        own_sums = back.reshape(2, most, width)
        spread = one_hot.T
        moe_out = (weight[:, None] * dot(spread, own_sums[0])).astype(BF16)
        grad_tokens = dot(spread, own_sums[1]).astype(BF16)
        return moe_out, grad_tokens

    return per_device


def call(body, outs, *args, scratch=(), us=0):
    return pl.pallas_call(
        body,
        out_shape=list(outs),
        scratch_shapes=list(scratch),
        compiler_params=pltpu.CompilerParams(vmem_limit_bytes=40 * 1024 * 1024),
        cost_estimate=pl.CostEstimate(flops=us * 1000000000, bytes_accessed=1024, transcendentals=0),
    )(*args)


def after(values, *others):
    return lax.optimization_barrier((values, *others))


def shaped(shape, kind):
    return jax.ShapeDtypeStruct(shape, kind)


def flip_pairs(values, own_width):
    parts = [values[..., i * own_width : (i + 1) * own_width] for i in (1, 0, 3, 2)]
    return jnp.concatenate(parts, axis=-1)


def route_columns(experts_ref, gates_ref):
    count = experts_ref.shape[0] // 4
    start = pl.multiple_of(lax.axis_index("et") * count, count)
    experts = experts_ref[pl.ds(start, count), :]
    gates = gates_ref[pl.ds(start, count), :]
    hits = (experts == 0).astype(F32)
    chosen = jnp.sum(hits, axis=1, keepdims=True)
    weight = jnp.sum(hits * gates, axis=1, keepdims=True)
    return chosen, weight


def as_row(column, keep):
    return jnp.sum(jnp.where(keep, column, 0.0), axis=0, keepdims=True)


def weight_chunk_body(low_ref, *refs):
    for gate, up, down, out in (refs[0:3] + refs[6:7], refs[3:6] + refs[7:8]):
        out[0] = gate[...]
        out[1] = up[...]
        out[2] = down[...].T


def weight_chunk(low, w_gate, w_up, w_down, lo, size):
    own_width, hidden_units = w_gate.shape
    half = hidden_units // 2 // size
    at = lo // size

    def spec(kept, rows):
        def index(i, low_ref):
            block = at + half * (low_ref[0] if kept else 1 - low_ref[0])
            return (block, 0) if rows else (0, block)

        return pl.BlockSpec((size, own_width) if rows else (own_width, size), index)

    out = shaped((3, own_width, size), BF16)
    specs = [spec(kept, rows) for kept in (True, False) for rows in (False, False, True)]
    whole = pl.BlockSpec((3, own_width, size), lambda i, low_ref: (0, 0, 0))
    return pl.pallas_call(
        weight_chunk_body,
        out_shape=[out, out],
        grid_spec=pltpu.PrefetchScalarGridSpec(
            num_scalar_prefetch=1, grid=(1,), in_specs=specs, out_specs=[whole, whole]
        ),
        compiler_params=pltpu.CompilerParams(vmem_limit_bytes=60 * 1024 * 1024),
        cost_estimate=pl.CostEstimate(
            flops=0, bytes_accessed=1024, transcendentals=0
        ),
    )(low, w_gate, w_up, w_down, w_gate, w_up, w_down)


def weight_part_body(low_ref, gate, up, down, out):
    out[0] = gate[...]
    out[1] = up[...]
    out[2] = down[...].T


def weight_part(low, w_gate, w_up, w_down, lo, size, kept):
    own_width, hidden_units = w_gate.shape
    half = hidden_units // 2 // size

    def block(low_ref):
        return lo // size + half * (low_ref[0] if kept else 1 - low_ref[0])

    across = pl.BlockSpec((own_width, size), lambda i, low_ref: (0, block(low_ref)))
    down = pl.BlockSpec((size, own_width), lambda i, low_ref: (block(low_ref), 0))
    out = shaped((3, own_width, size), BF16)
    return pl.pallas_call(
        weight_part_body,
        out_shape=out,
        grid_spec=pltpu.PrefetchScalarGridSpec(
            num_scalar_prefetch=1,
            grid=(1,),
            in_specs=[across, across, down],
            out_specs=pl.BlockSpec(out.shape, lambda i, low_ref: (0, 0, 0)),
        ),
        compiler_params=pltpu.CompilerParams(vmem_limit_bytes=60 * 1024 * 1024),
        cost_estimate=pl.CostEstimate(flops=0, bytes_accessed=1024, transcendentals=0),
    )(low, w_gate, w_up, w_down)


def make_fused(n_fsdp, n_et):
    world = n_fsdp * n_et

    def swap(values, mask):
        pairs = [(i, i ^ mask) for i in range(world)]
        return lax.ppermute(values, ("fsdp", "et"), pairs)

    at_y, at_zp, at_zh = n_et, 2 * n_et, 4 * n_et
    at_core, at_x = 1, 2

    def per_device(tokens, cotangent, route_experts, route_gates, w_gate, w_up, w_down):
        own_count, width = tokens.shape
        most = own_count // 8
        own_width, hidden_units = w_gate.shape
        half_units = hidden_units // 2
        z_width = 4 * own_width
        block_shape = (2, most, z_width)
        low = ((lax.axis_index("fsdp") // 2) % 2).astype(jnp.int32).reshape(1)

        chunks = chunk_list(half_units)
        count = len(chunks)
        own_w, zp_w = [None] * count, [None] * count
        given = [None] * count

        stream = []

        def over_y(values):
            stream.append(swap(values, at_y))

        for k in range(count):
            if k == 0:
                own_w[0] = weight_part(low, w_gate, w_up, w_down, *chunks[0], True)
                given[0] = weight_part(low, w_gate, w_up, w_down, *chunks[0], False)
                continue
            own_w[k], given[k] = weight_chunk(low, w_gate, w_up, w_down, *chunks[k])
        over_y(own_w[0])
        zp_w[0] = swap(given[0], at_zp)
        over_y(own_w[1])

        def pack_body(tokens_ref, cot_ref, experts_ref, gates_ref, keep_ref, send_ref, packed_ref):
            chosen, weight = route_columns(experts_ref, gates_ref)
            shape = (own_count, own_count)
            down = lax.broadcasted_iota(jnp.int32, shape, 0)
            across = lax.broadcasted_iota(jnp.int32, shape, 1)
            chosen_row = as_row(chosen, down == across)
            weight_row = as_row(weight, down == across)
            slot_row = as_row(chosen, down < across)
            places = lax.broadcasted_iota(jnp.int32, (most, own_count), 0).astype(F32)
            picks = jnp.logical_and(slot_row == places, chosen_row > 0.0)
            one_hot = jnp.where(picks, 1.0, 0.0).astype(BF16)
            slot_weight = jnp.sum(jnp.where(picks, weight_row, 0.0), axis=1, keepdims=True)
            packed_ref[0] = dot(one_hot, tokens_ref[...]).astype(BF16)
            packed_ref[1] = (slot_weight * dot(one_hot, cot_ref[...])).astype(BF16)
            f_index = lax.axis_index("fsdp")
            for d, out in enumerate((keep_ref, send_ref)):
                for i in range(4):
                    mask = 4 * d + 2 * (i % 2) + i // 2
                    start = pl.multiple_of((f_index ^ mask) * own_width, LANES)
                    columns = slice(i * own_width, (i + 1) * own_width)
                    out[:, :, columns] = packed_ref[:, :, pl.ds(start, own_width)]

        block = shaped(block_shape, BF16)
        mine, sent = call(
            pack_body,
            [block, block],
            tokens,
            cotangent,
            route_experts,
            route_gates,
            scratch=[pltpu.VMEM((2, most, width), BF16)],
        )
        other = swap(sent, at_zh)

        def join_body(mine_ref, other_ref, plain_ref, flipped_ref):
            for j, ref in enumerate((mine_ref, other_ref)):
                values = ref[...]
                plain_ref[j] = values
                flipped_ref[j] = flip_pairs(values, own_width)

        pair = shaped((2,) + block_shape, BF16)
        mine, stream[0] = after(mine, stream[0])
        mine, zp_w[0] = after(mine, zp_w[0])
        plain, flipped = call(join_body, [pair, pair], mine, other)
        own_w[2], _ = after(own_w[2], plain)
        over_y(zp_w[0])
        over_y(own_w[2])
        for k, first_done in ((1, sent), (2, plain)):
            given[k], _ = after(given[k], first_done)
            zp_w[k] = swap(given[k], at_zp)
        near_rows = jnp.stack(
            [plain, swap(plain, at_x), swap(flipped, at_zp), swap(flipped, at_zp + at_x)]
        )
        near_rows, stream[1] = after(near_rows, stream[1])
        far_rows = swap(near_rows, at_core)
        near_rows, stream[3] = after(near_rows, stream[3])
        near_rows, zp_w[1] = after(near_rows, zp_w[1])
        over_y(zp_w[1])

        slots = 16 * most
        own_slots = slots // 2

        def rows_of(near_ref, far_ref, which):
            parts = [ref[:, :, which].reshape(own_slots, z_width) for ref in (near_ref, far_ref)]
            return jnp.concatenate(parts, axis=0)

        def first_body(near_ref, far_ref, a_ref, b_ref, c_ref, d_ref, keep_ref, send_ref):
            units = a_ref.shape[2]
            rows = rows_of(near_ref, far_ref, 0)
            cots = rows_of(near_ref, far_ref, 1)
            for j in range(3):
                left = cots if j == 2 else rows
                value = None
                for i, ref in enumerate((a_ref, b_ref, c_ref, d_ref)):
                    term = dot(left[:, i * own_width : (i + 1) * own_width], ref[j])
                    value = term if value is None else value + term
                columns = slice(j * units, (j + 1) * units)
                keep_ref[:, columns] = value
                value = value.astype(BF16).reshape(8, 2, most, units)
                value = jnp.concatenate([value[:, 1:2], value[:, 0:1]], axis=1)
                send_ref[:, columns] = value.reshape(slots, units)

        def second_terms(keep_ref, recv_ref, refs):
            units = refs[0].shape[2]
            pre = keep_ref[...] + recv_ref[...].astype(F32)
            gate, up, grad = pre[:, :units], pre[:, units : 2 * units], pre[:, 2 * units :]
            sig = 1.0 / (1.0 + jnp.exp(-gate))
            hidden = (gate * sig * up).astype(BF16)
            grad_gate = (grad * up * sig * (1.0 + gate * (1.0 - sig))).astype(BF16)
            grad_up = (grad * gate * sig).astype(BF16)
            outs = [dot_last(hidden, ref[2]) for ref in refs]
            grads = [dot_last(grad_gate, ref[0]) + dot_last(grad_up, ref[1]) for ref in refs]
            return outs, grads

        def second_body(first, last, keep_ref, recv_ref, a_ref, b_ref, c_ref, d_ref, *rest):
            terms = second_terms(keep_ref, recv_ref, (a_ref, b_ref, c_ref, d_ref))
            rest = list(rest)
            held = None if first else rest.pop(0)
            for which in range(2):
                for i in range(4):
                    columns = slice(i * own_width, (i + 1) * own_width)
                    value = terms[which][i]
                    if held is not None:
                        value = value + held[which, :, columns]
                    if not last:
                        rest[0][which, :, columns] = value
                        continue
                    value = value.reshape(2, 4, 2, most, own_width)
                    for j in range(2):
                        rest[0][:, j, which, :, columns] = value[0, :, j]
                        rest[1][:, j, which, :, columns] = value[1, :, j].astype(BF16)

        quad = (4, 2) + block_shape
        pre, total = [None] * count, [None] * count

        def weights_of(k):
            at = ((0, 2), (1, 4), (3, 5))[k] if k < 3 else (2 * k, 2 * k + 1)
            return own_w[k], zp_w[k], stream[at[0]], stream[at[1]]

        def first(k, near_rows, far_rows):
            units = chunks[k][1]
            pre[k] = call(
                first_body,
                [shaped((slots, 3 * units), F32), shaped((slots, 3 * units), BF16)],
                near_rows,
                far_rows,
                *weights_of(k),
                us=8 * units // 256,
            )

        def second(k):
            is_first, is_last = k == 0, k == count - 1
            outs = (
                [shaped(quad, F32), shaped(quad, BF16)]
                if is_last
                else [shaped((2, slots, z_width), F32)]
            )
            held = () if is_first else total[k - 1]
            keep, sent = pre[k]
            total[k] = call(
                lambda *refs: second_body(is_first, is_last, *refs),
                outs,
                keep,
                swap(sent, at_zh),
                *weights_of(k),
                *held,
            )

        def held_back(values, firsts=(), seconds=()):
            done = [pre[k][1] for k in firsts] + [total[k][0] for k in seconds]
            if not done:
                return values
            values, *done = after(values, *done)
            for k in firsts:
                pre[k] = [pre[k][0], done.pop(0)]
            for k in seconds:
                total[k] = [done.pop(0)]
            return values

        def first_after(k, *steps):
            first(k, held_back(near_rows, *steps), far_rows)

        def second_after(k, *steps):
            pre[k] = [held_back(pre[k][0], *steps), pre[k][1]]
            second(k)

        def pair_exchange(k, *steps):
            given[k] = held_back(given[k], *steps)
            zp_w[k] = swap(given[k], at_zp)

        def own_over_y(k, *steps):
            own_w[k] = held_back(own_w[k], *steps)
            over_y(own_w[k])

        def pair_over_y(k, *steps):
            zp_w[k] = held_back(zp_w[k], *steps)
            over_y(zp_w[k])

        first(0, near_rows, far_rows)
        pair_exchange(3, [0])
        pair_over_y(2, [0])
        first_after(1, [0])
        pair_exchange(4, [1])
        own_over_y(3, [1])
        pair_over_y(3, [1])
        second_after(0, [1])
        first_after(2, [1])
        pair_exchange(5, [2])
        own_over_y(4, [2])
        pair_over_y(4, [2])
        second_after(1, [2])
        first_after(3, [], [0])
        own_over_y(5, [3])
        pair_over_y(5, [3])
        second(2)
        first_after(4, [3], [1])
        second_after(3, [4])
        first_after(5, [4], [3])
        second_after(4, [5])
        second(5)
        total = total[-1]

        def spread_body(keep_ref, recv_ref, own_ref, *outs):
            value = keep_ref[...] + recv_ref[...].astype(F32)
            own_ref[...] = value[0]
            for i in range(1, 4):
                part = value[i].astype(BF16)
                outs[i - 1][...] = flip_pairs(part, own_width) if i >= 2 else part

        keep, sent = total
        own, by_x, by_zp, by_both = call(
            spread_body,
            [shaped(pair.shape, F32), pair, pair, pair],
            keep,
            swap(sent, at_core),
        )

        def gather_body(own_ref, x_ref, zp_ref, both_ref, keep_ref, send_ref):
            value = own_ref[...] + x_ref[...].astype(F32)
            value = value + (zp_ref[...].astype(F32) + both_ref[...].astype(F32))
            keep_ref[...] = value[0].astype(BF16)
            send_ref[...] = value[1].astype(BF16)

        mine, sent = call(
            gather_body,
            [block, block],
            own,
            swap(by_x, at_x),
            swap(by_zp, at_zp),
            swap(by_both, at_zp + at_x),
        )

        def unpack_body(mine_ref, other_ref, experts_ref, gates_ref, out_ref, grad_ref, sums_ref):
            f_index = lax.axis_index("fsdp")
            for d, ref in enumerate((mine_ref, other_ref)):
                for i in range(4):
                    mask = 4 * d + 2 * (i % 2) + i // 2
                    start = pl.multiple_of((f_index ^ mask) * own_width, LANES)
                    columns = slice(i * own_width, (i + 1) * own_width)
                    sums_ref[:, :, pl.ds(start, own_width)] = ref[:, :, columns]
            chosen, weight = route_columns(experts_ref, gates_ref)
            shape = (own_count, own_count)
            down = lax.broadcasted_iota(jnp.int32, shape, 0)
            across = lax.broadcasted_iota(jnp.int32, shape, 1)
            chosen_row = as_row(chosen, down == across)
            slot = jnp.sum(jnp.where(across < down, chosen_row, 0.0), axis=1, keepdims=True)
            places = lax.broadcasted_iota(jnp.int32, (own_count, most), 1).astype(F32)
            picks = jnp.logical_and(slot == places, chosen > 0.0)
            spread = jnp.where(picks, 1.0, 0.0).astype(BF16)
            out_ref[...] = (weight * dot(spread, sums_ref[0])).astype(BF16)
            grad_ref[...] = dot(spread, sums_ref[1]).astype(BF16)

        result = shaped(tokens.shape, BF16)
        return tuple(
            call(
                unpack_body,
                [result, result],
                mine,
                swap(sent, at_zh),
                route_experts,
                route_gates,
                scratch=[pltpu.VMEM((2, most, width), BF16)],
                )
        )

    return per_device


def solution(mesh):
    sizes = dict(mesh.shape)
    make = make_fused if sizes["fsdp"] == 8 and sizes["et"] == 4 else make_plain
    in_specs = (
        P(("fsdp", "et"), None),
        P(("fsdp", "et"), None),
        P("fsdp", None),
        P("fsdp", None),
        P("fsdp", "et"),
        P("fsdp", "et"),
        P("et", "fsdp"),
    )
    out_specs = (P(("fsdp", "et"), None), P(("fsdp", "et"), None))
    return jax.shard_map(
        make(sizes["fsdp"], sizes["et"]),
        mesh=mesh,
        in_specs=in_specs,
        out_specs=out_specs,
        check_vma=False,
    )
```
